512 devices in a mesh: stack: 64 (over x, z_lo, core), rows: 8 (over z_hi, y).
Axes of the slice: x: 4, y: 4, z: 16 (z_hi: 2, z_lo: 8; z = z_hi * 8 + z_lo), core: 2. Of those that a mesh axis runs over, the one named last changes fastest.
Arguments:
- interferograms: float32 [1024, 512, 1024], P('stack', 'rows'), may hold values from -48 to 48
- pairs: int32 [1024, 2], replicated, may hold values from 0 to 191, as said below
Outputs:
- filtered: float32 [192, 512, 1024], P('stack', 'rows')
The draws below stay inside these ranges and needn't reach their ends.
Inputs may be any that keep to these rules, and one draw needn't show every extreme that they name: `pairs`: row k holds the reference date and then the secondary date of interferogram k, with reference < secondary <= reference + 24.
All inputs are finite; a program needn't handle non-finite values.
Results may differ from the reference program's by a relative error of at most 0.00007.
Values sent between devices are 32-bit elements; how exact they have to be, the bound alone decides.
A program may use at most 128 MiB of HBM per device.

```python
import jax
import jax.numpy as jnp
from jax import lax

M = 1024
ND = 192
GAP = 24
R = 4
W = 1024
H = 512


def draw_pairs(key, part):
    first_key, second_key = jax.random.split(key)
    reference_dates = jax.random.randint(first_key, (M,), 0, ND - 1)
    date_gaps = jax.random.randint(second_key, (M,), 1, GAP + 1)
    position = jnp.arange(M)
    reference_dates = jnp.where(position == 0, 0, reference_dates)
    reference_dates = jnp.where(position == 1, ND - 2, reference_dates)
    secondary = jnp.minimum(reference_dates + date_gaps, ND - 1)
    return jnp.stack([reference_dates, secondary], axis=1).astype(jnp.int32)


def levels(rng, shape, shards, low, top_value):
    loudness = 1.0
    for dim, blocks in shards:
        heights = jax.random.uniform(jax.random.fold_in(jax.random.fold_in(rng, 6), dim), (blocks,), jnp.float32, low / len(shards), top_value / len(shards))
        loudness = loudness * jnp.repeat(jnp.exp(heights), shape[dim] // blocks).reshape((-1,) + (1,) * (len(shape) - 1 - dim))
    return loudness


def scatter_about(stream_key, shape, spread, most, pieces=(), kind=jnp.bfloat16):
    factor_of = levels(stream_key, shape, pieces, -0.22, 0.18) if pieces else 1.0
    array = jax.random.normal(stream_key, shape, jnp.float32) * spread * factor_of
    return jnp.minimum(jnp.maximum(array, -most), most).astype(kind)


def setup_inputs(seed: int = 0) -> dict:
    seeds = jax.random.split(jax.random.key(seed), 3)
    interferograms = scatter_about(seeds[0], (M, H, W), 8.0, 48.0, ((0, 64), (1, 8)), jnp.float32)
    pairs = draw_pairs(jax.random.fold_in(seeds[2], 71), 0)
    return {"interferograms": interferograms, "pairs": pairs}


TIKHONOV = 0.1
TEMPORAL_SIGMA = 6.0
SPATIAL_SIGMA = 1.5

def build_tables(pairs, date_total):
    date_index = jnp.arange(date_total, dtype=jnp.int32)
    design = (pairs[:, 1:2] == date_index[None, :]).astype(jnp.float32) - (pairs[:, 0:1] == date_index[None, :]).astype(jnp.float32)
    normal = jnp.dot(design.T.astype(jnp.float32), design.astype(jnp.float32), precision=lax.Precision.HIGHEST, preferred_element_type=jnp.float32)
    normal = normal + TIKHONOV * jnp.eye(date_total, dtype=jnp.float32)
    factor = jnp.linalg.cholesky(normal)
    pseudo = jax.scipy.linalg.cho_solve((factor, True), design.T)
    offsets = (date_index[:, None] - date_index[None, :]).astype(jnp.float32) / TEMPORAL_SIGMA
    kernel = jnp.exp(-0.5 * offsets * offsets)
    smooth = kernel / jnp.sum(kernel, axis=1, keepdims=True)
    return (pseudo, smooth)

def spatial_taps(radius):
    offsets = jnp.arange(-radius, radius + 1).astype(jnp.float32) / SPATIAL_SIGMA
    kernel = jnp.exp(-0.5 * offsets * offsets)
    return kernel / jnp.sum(kernel)

def along_rows(padded, height, weights):
    summed = weights[0] * padded[:, 0:height, :]
    for position in range(1, weights.shape[0]):
        summed = summed + weights[position] * padded[:, position:position + height, :]
    return summed

def along_columns(padded, length, weights):
    summed = weights[0] * padded[:, :, 0:length]
    for position in range(1, weights.shape[0]):
        summed = summed + weights[position] * padded[:, :, position:position + length]
    return summed

def reference(interferograms, pairs):
    stack_depth, image_height, image_width = interferograms.shape
    pseudo, smooth = build_tables(pairs, ND)
    flattened = interferograms.reshape(stack_depth, image_height * image_width)
    displacement = jnp.dot(pseudo.astype(jnp.float32), flattened.astype(jnp.float32), precision=lax.Precision.HIGHEST, preferred_element_type=jnp.float32)
    highpass = displacement - jnp.dot(smooth.astype(jnp.float32), displacement.astype(jnp.float32), precision=lax.Precision.HIGHEST, preferred_element_type=jnp.float32)
    date_field = highpass.reshape(ND, image_height, image_width)
    weights = spatial_taps(R)
    padded = jnp.pad(date_field, ((0, 0), (R, R), (0, 0)))
    rowpass = along_rows(padded, image_height, weights)
    widened = jnp.pad(rowpass, ((0, 0), (0, 0), (R, R)))
    return along_columns(widened, image_width, weights)
```

```python
import functools

import jax
import jax.numpy as jnp
import numpy as np
from jax import lax
from jax.experimental import pallas as pl
from jax.experimental.pallas import tpu as pltpu
from jax.sharding import PartitionSpec as P

ND = 192
R = 4
TIKHONOV = 0.1
TEMPORAL_SIGMA = 6.0
SPATIAL_SIGMA = 1.5

LINE = 8
OWNERS = 8
DEPTH = 16
LANES = 128
CHUNKS = 8
SHARE = ND // LINE
KEEP = ND // (LINE * OWNERS)
PAD = 256
GROUP = 2
LAG = 3
ROUNDS = 9
f32 = jnp.float32
bf16 = jnp.bfloat16


def spatial_taps():
    offsets = np.arange(-R, R + 1).astype(np.float32) / np.float32(SPATIAL_SIGMA)
    taps = np.exp(np.float32(-0.5) * offsets * offsets)
    return [float(tap) for tap in (taps / np.sum(taps)).astype(np.float32)]


def dot(a, b):
    return jnp.dot(a, b, preferred_element_type=f32)


def two(a):
    high = a.astype(bf16)
    return high, (a - high.astype(f32)).astype(bf16)


def dot3(a, b):
    ah, al = two(a)
    bh, bl = two(b)
    return dot(ah, bh) + (dot(ah, bl) + dot(al, bh))


def dot6(a, b):
    return jnp.dot(a, b, precision=lax.Precision.HIGHEST, preferred_element_type=f32)


def inverse(normal, eye, ex):
    top = jnp.max(jnp.sum(jnp.abs(normal), axis=1, keepdims=True), axis=0, keepdims=True)
    scale = 2.0 / (top + TIKHONOV)
    ex[0:PAD] = eye - scale * normal
    ex[PAD : 2 * PAD] = scale * eye

    def turn(_, rho):
        both = ex[...]
        err = both[0:PAD]
        product = dot3(both, err)
        gain = 2.0 / (2.0 - rho * rho)
        ex[0:PAD] = gain * product[0:PAD] + (1.0 - gain) * eye
        ex[PAD : 2 * PAD] = gain * (both[PAD : 2 * PAD] + product[PAD : 2 * PAD])
        return 0.5 * rho * rho * gain

    lax.fori_loop(0, ROUNDS, turn, (top - TIKHONOV) / (top + TIKHONOV))

    def polish(_, carry):
        now = ex[PAD : 2 * PAD]
        left = eye - dot6(normal, now)
        ex[PAD : 2 * PAD] = now + dot3(now, left)
        return carry

    lax.fori_loop(0, 3, polish, 0)
    return ex[PAD : 2 * PAD]


def tables(z, pairs, ex, q_high, q_low):
    dates = lax.broadcasted_iota(jnp.int32, (PAD, pairs.shape[1]), 0)
    design = (dates == pairs[1:2, :]).astype(f32) - (dates == pairs[0:1, :]).astype(f32)
    design = design.astype(bf16)
    row = lax.broadcasted_iota(jnp.int32, (PAD, PAD), 0)
    col = lax.broadcasted_iota(jnp.int32, (PAD, PAD), 1)
    eye = (row == col).astype(f32)
    normal = lax.dot_general(design, design, (((1,), (1,)), ((), ())), preferred_element_type=f32)
    normal = normal + TIKHONOV * eye
    solved = inverse(normal, eye, ex)
    at_z = (row * 2731) >> 16
    rest = row - SHARE * at_z
    at_x = (rest * 43) >> 8
    date = 48 * at_x + 6 * at_z + (rest - 6 * at_x)
    offset = (date - col).astype(f32) / TEMPORAL_SIGMA
    weight = jnp.where(col < ND, jnp.exp(-0.5 * offset * offset), 0.0)
    smooth = weight / jnp.sum(weight, axis=1, keepdims=True)
    change = dot6((date == col).astype(f32) - smooth, solved)
    k = lax.broadcasted_iota(jnp.int32, (pairs.shape[1], LANES), 0)
    j = lax.broadcasted_iota(jnp.int32, (pairs.shape[1], LANES), 1)
    pick = (k == 256 * (j >> 5) + 32 * z + (j & 31)).astype(f32).astype(bf16)
    mine = dot(design, pick).astype(bf16)
    first = change.astype(bf16)
    rest = change - first.astype(f32)
    second = rest.astype(bf16)
    third = (rest - second.astype(f32)).astype(bf16)
    q = dot(first, mine) + (dot(second, mine) + dot(third, mine))
    high, low = two(q[0:ND])
    q_high[...] = jnp.concatenate([high, high], axis=1)
    q_low[...] = low


def kernel(
    ifg, pairs, out, x_buf, p_buf, r_buf, l_buf, fin, fr, ex, q_high, q_low,
    x_send, x_recv, r_send, r_recv, l_send, l_recv, f_send, f_recv, h_send, h_recv,
):
    stack = lax.axis_index("stack")
    slab = lax.axis_index("rows")
    slabs = lax.axis_size("rows")
    x = stack // (2 * LINE)
    z = (stack // 2) % LINE
    core = stack % 2
    me = 2 * x + core
    mirror = LINE - 1 - z
    half = z // (LINE // 2)
    near = z * (1 - half) + mirror * half
    wait_for = near + LAG * (LINE - 1 - near)

    def peer(owner):
        return {"stack": 2 * LINE * (owner // 2) + 2 * z + owner % 2}

    def remote(src, dst, send, recv, device):
        return pltpu.make_async_remote_copy(
            src_ref=src, dst_ref=dst, send_sem=send, recv_sem=recv,
            device_id=device, device_id_type=pl.DeviceIdType.MESH,
        )

    def landed(ref, sem):
        pltpu.make_async_copy(ref, ref, sem).wait()

    right = {"stack": stack + 2}
    left = {"stack": stack - 2}
    below = {"rows": slab + 1}
    above = {"rows": slab - 1}
    has_left, has_right = z > 0, z < LINE - 1
    has_above, has_below = slab > 0, slab < slabs - 1

    barrier = pltpu.get_barrier_semaphore()

    def greet(device):
        pl.semaphore_signal(barrier, inc=1, device_id=device, device_id_type=pl.DeviceIdType.MESH)

    for step in range(1, OWNERS):
        greet(peer((me + step) % OWNERS))
    for there, device in ((has_left, left), (has_right, right), (has_above, above), (has_below, below)):
        pl.when(there)(functools.partial(greet, device))
    count = OWNERS - 1 + (z + LINE - 1) // LINE + (mirror + LINE - 1) // LINE
    count = count + (slab + slabs - 1) // slabs + (2 * slabs - 2 - slab) // slabs
    pl.semaphore_wait(barrier, count)

    def x_piece(c, owner):
        rows = pl.ds(pl.multiple_of(8 * ((c + CHUNKS - 1) % CHUNKS), 8), 8)
        return ifg.at[:, rows, pl.ds(pl.multiple_of(LANES * owner, LANES), LANES)]

    def x_slot(c):
        return x_buf.at[c, pl.ds(DEPTH * me, DEPTH)]

    def spread(c, carry):
        for step in range(1, OWNERS):
            owner = (me + step) % OWNERS
            remote(x_piece(c, owner), x_slot(c), x_send.at[c], x_recv.at[c], peer(owner)).start()
        pltpu.make_async_copy(x_piece(c, me), x_slot(c), x_recv.at[c]).start()
        return carry

    lax.fori_loop(0, CHUNKS, spread, 0)

    tables(z, pairs, ex, q_high, q_low)

    @pl.when(jnp.logical_not(has_above))
    def _():
        fr[0] = jnp.zeros(fr.shape[1:], f32)

    @pl.when(jnp.logical_not(has_below))
    def _():
        fr[CHUNKS + 1] = jnp.zeros(fr.shape[1:], f32)

    taps = spatial_taps()

    def compute(c):
        landed(x_buf.at[c], x_recv.at[c])
        for s in range(0, 8, 2):
            block = jnp.concatenate([x_buf[c, :, s], x_buf[c, :, s + 1]], axis=1)
            high, low = two(block)
            product = dot(q_high[...], jnp.concatenate([high, low], axis=0)) + dot(q_low[...], high)
            for t in range(2):
                p_buf[c, :, s + t] = product[:, LANES * t : LANES * (t + 1)].reshape(LINE, SHARE, LANES)

    def collect(c):
        for s in range(8):
            fin[c, :, s] = p_buf[c, z, s]
        for step in range(1, OWNERS):
            owner = (me + step) % OWNERS
            remote(
                fin.at[c, pl.ds(KEEP * owner, KEEP)], fr.at[(c + CHUNKS - 1) % CHUNKS + 1, me],
                f_send.at[c], f_recv.at[c], peer(owner),
            ).start()
        pltpu.make_async_copy(
            fin.at[c, pl.ds(KEEP * me, KEEP)], fr.at[(c + CHUNKS - 1) % CHUNKS + 1, me], f_recv.at[c]
        ).start()

    def low_pass(q):
        lane = lax.broadcasted_iota(jnp.int32, (8, LANES * OWNERS), 1)
        for i in range(KEEP):
            window = jnp.concatenate(
                [fr[q, :, i, 8 - R : 8], fr[q + 1, :, i], fr[q + 2, :, i, 0:R]], axis=1
            )
            rowpass = taps[R] * window[:, R : R + 8]
            for s in range(1, R + 1):
                rowpass = rowpass + taps[R + s] * (
                    window[:, R - s : R - s + 8] + window[:, R + s : R + s + 8]
                )
            line = jnp.concatenate([rowpass[o] for o in range(OWNERS)], axis=1)
            total = taps[R] * line
            width = LANES * OWNERS
            for s in range(1, R + 1):
                before = jnp.where(lane >= s, pltpu.roll(line, s, 1), 0.0)
                after = jnp.where(lane < width - s, pltpu.roll(line, width - s, 1), 0.0)
                total = total + taps[R + s] * (before + after)
            out[i, pl.ds(pl.multiple_of(8 * q, 8), 8)] = total

    halo_down = remote(
        fr.at[CHUNKS, :, :, pl.ds(8 - R, R)], fr.at[0, :, :, pl.ds(8 - R, R)], h_send.at[0], h_recv.at[0], below
    )
    halo_up = remote(
        fr.at[1, :, :, pl.ds(0, R)], fr.at[CHUNKS + 1, :, :, pl.ds(0, R)], h_send.at[1], h_recv.at[1], above
    )

    def finish(c):
        landed(fr.at[(c + CHUNKS - 1) % CHUNKS + 1], f_recv.at[c])

        @pl.when((c == 0) & has_below)
        def _():
            halo_down.start()

        @pl.when((c == 1) & has_above)
        def _():
            halo_up.start()

        @pl.when(c >= 3)
        def _():
            low_pass(c - 2)

    span = (LINE - 1) * GROUP
    items = (LINE - 1) * CHUNKS

    def place(item):
        group = item // span
        rest = item % span
        return GROUP * group + rest % GROUP, rest // GROUP

    def step(t, carry):
        at = t - LAG * near

        @pl.when((at >= 0) & (at < items))
        def _():
            c, hop = place(at)

            @pl.when(hop == 0)
            def _():
                compute(c)

        at_right = t - LAG * z

        @pl.when((at_right >= 0) & (at_right < items))
        def _():
            c, hop = place(at_right)
            d = LINE - 1 - hop

            @pl.when((d >= z) & has_left)
            def _():
                landed(r_buf.at[c, d], r_recv.at[c, d])
                p_buf[c, d] = p_buf[c, d] + r_buf[c, d]

            @pl.when(d > z)
            def _():
                remote(p_buf.at[c, d], r_buf.at[c, d], r_send.at[c, d], r_recv.at[c, d], right).start()

        at_left = t - LAG * mirror

        @pl.when((at_left >= 0) & (at_left < items))
        def _():
            c, d = place(at_left)

            @pl.when((d <= z) & has_right)
            def _():
                landed(l_buf.at[c, d], l_recv.at[c, d])
                p_buf[c, d] = p_buf[c, d] + l_buf[c, d]

            @pl.when(d < z)
            def _():
                remote(p_buf.at[c, d], l_buf.at[c, d], l_send.at[c, d], l_recv.at[c, d], left).start()

        at_end = t - (GROUP * near + LAG * (LINE - 1 - near))

        @pl.when((at_end >= 0) & (at_end < items))
        def _():
            c, hop = place(at_end)

            @pl.when(hop == 0)
            def _():
                collect(c)

        at_out = at_end - LAG

        @pl.when((at_out >= 0) & (at_out < items))
        def _():
            c, hop = place(at_out)

            @pl.when(hop == 0)
            def _():
                finish(c)

        return carry

    steps = items + (LINE - 1) * max(LAG, GROUP) + LAG
    lax.fori_loop(0, steps, step, 0)

    @pl.when(has_above)
    def _():
        halo_down.wait_recv()
        halo_up.wait_send()

    @pl.when(has_below)
    def _():
        halo_up.wait_recv()
        halo_down.wait_send()

    def tail(q, carry):
        low_pass(q)
        return carry

    low_pass(0)
    lax.fori_loop(CHUNKS - 2, CHUNKS, tail, 0)

    def drain(c, carry):
        landed(x_buf.at[c, pl.ds(0, (OWNERS - 1) * DEPTH)], x_send.at[c])
        landed(fr.at[1, pl.ds(0, OWNERS - 1)], f_send.at[c])

        def each(d, carry):
            @pl.when(d > z)
            def _():
                landed(p_buf.at[c, d], r_send.at[c, d])

            @pl.when(d < z)
            def _():
                landed(p_buf.at[c, d], l_send.at[c, d])

            return carry

        return lax.fori_loop(0, LINE, each, carry)

    lax.fori_loop(0, CHUNKS, drain, 0)


def shards(interferograms, pairs):
    dma = pltpu.SemaphoreType.DMA
    block = (CHUNKS, LINE, 8, SHARE, LANES)
    return pl.pallas_call(
        kernel,
        out_shape=jax.ShapeDtypeStruct((KEEP,) + interferograms.shape[1:], f32),
        in_specs=[pl.BlockSpec(memory_space=pltpu.HBM), pl.BlockSpec(memory_space=pltpu.VMEM)],
        out_specs=pl.BlockSpec(memory_space=pltpu.VMEM),
        scratch_shapes=[
            pltpu.VMEM((CHUNKS, DEPTH * OWNERS, 8, LANES), f32),
            pltpu.VMEM(block, f32),
            pltpu.VMEM(block, f32),
            pltpu.VMEM(block, f32),
            pltpu.VMEM((CHUNKS, SHARE, 8, LANES), f32),
            pltpu.VMEM((CHUNKS + 2, OWNERS, KEEP, 8, LANES), f32),
            pltpu.VMEM((2 * PAD, PAD), f32),
            pltpu.VMEM((ND, 2 * LANES), bf16),
            pltpu.VMEM((ND, LANES), bf16),
            dma((CHUNKS,)), dma((CHUNKS,)),
            dma((CHUNKS, LINE)), dma((CHUNKS, LINE)),
            dma((CHUNKS, LINE)), dma((CHUNKS, LINE)),
            dma((CHUNKS,)), dma((CHUNKS,)),
            dma((2,)), dma((2,)),
        ],
        compiler_params=pltpu.CompilerParams(
            collective_id=0, has_side_effects=True, vmem_limit_bytes=48 * 1024 * 1024
        ),
    )(interferograms, pairs.T)


def solution(mesh):
    return jax.shard_map(
        shards,
        mesh=mesh,
        in_specs=(P("stack", "rows", None), P()),
        out_specs=P("stack", "rows", None),
        check_vma=False,
    )
```

```python
import functools

import jax
import jax.numpy as jnp
import numpy as np
from jax import lax
from jax.experimental import pallas as pl
from jax.experimental.pallas import tpu as pltpu
from jax.sharding import PartitionSpec as P

ND = 192
R = 4
TIKHONOV = 0.1
TEMPORAL_SIGMA = 6.0
SPATIAL_SIGMA = 1.5

LINE = 8
OWNERS = 8
DEPTH = 16
LANES = 128
BANDS = 8
CHUNKS = 16
HALF = 4
SHARE = ND // LINE
KEEP = ND // (LINE * OWNERS)
PAD = 256
WHOLE = 8
LAG = 6
AHEAD = 4
ROUNDS = 9
f32 = jnp.float32
bf16 = jnp.bfloat16


def spatial_taps():
    offsets = np.arange(-R, R + 1).astype(np.float32) / np.float32(SPATIAL_SIGMA)
    taps = np.exp(np.float32(-0.5) * offsets * offsets)
    return [float(tap) for tap in (taps / np.sum(taps)).astype(np.float32)]


def dot(a, b):
    return jnp.dot(a, b, preferred_element_type=f32)


def two(a):
    high = a.astype(bf16)
    return high, (a - high.astype(f32)).astype(bf16)


def dot3(a, b):
    ah, al = two(a)
    bh, bl = two(b)
    return dot(ah, bh) + (dot(ah, bl) + dot(al, bh))


def dot6(a, b):
    return jnp.dot(a, b, precision=lax.Precision.HIGHEST, preferred_element_type=f32)


def inverse(normal, eye, ex):
    top = jnp.max(jnp.sum(jnp.abs(normal), axis=1, keepdims=True), axis=0, keepdims=True)
    scale = 2.0 / (top + TIKHONOV)
    ex[0:PAD] = eye - scale * normal
    ex[PAD : 2 * PAD] = scale * eye

    def turn(_, rho):
        both = ex[...]
        err = both[0:PAD]
        product = dot3(both, err)
        gain = 2.0 / (2.0 - rho * rho)
        ex[0:PAD] = gain * product[0:PAD] + (1.0 - gain) * eye
        ex[PAD : 2 * PAD] = gain * (both[PAD : 2 * PAD] + product[PAD : 2 * PAD])
        return 0.5 * rho * rho * gain

    lax.fori_loop(0, ROUNDS, turn, (top - TIKHONOV) / (top + TIKHONOV))

    def polish(_, carry):
        now = ex[PAD : 2 * PAD]
        left = eye - dot6(normal, now)
        ex[PAD : 2 * PAD] = now + dot3(now, left)
        return carry

    lax.fori_loop(0, 3, polish, 0)
    return ex[PAD : 2 * PAD]


def tables(z, end, next_to_end, pairs, ex, q_high, q_low, e_high, e_low):
    dates = lax.broadcasted_iota(jnp.int32, (PAD, pairs.shape[1]), 0)
    design = (dates == pairs[1:2, :]).astype(f32) - (dates == pairs[0:1, :]).astype(f32)
    design = design.astype(bf16)
    row = lax.broadcasted_iota(jnp.int32, (PAD, PAD), 0)
    col = lax.broadcasted_iota(jnp.int32, (PAD, PAD), 1)
    eye = (row == col).astype(f32)
    normal = lax.dot_general(design, design, (((1,), (1,)), ((), ())), preferred_element_type=f32)
    normal = normal + TIKHONOV * eye
    solved = inverse(normal, eye, ex)
    at_z = (row * 2731) >> 16
    rest = row - SHARE * at_z
    at_x = (rest * 43) >> 8
    date = 48 * at_x + 6 * at_z + (rest - 6 * at_x)
    offset = (date - col).astype(f32) / TEMPORAL_SIGMA
    weight = jnp.where(col < ND, jnp.exp(-0.5 * offset * offset), 0.0)
    smooth = weight / jnp.sum(weight, axis=1, keepdims=True)
    change = dot6((date == col).astype(f32) - smooth, solved)
    first = change.astype(bf16)
    rest = change - first.astype(f32)
    second = rest.astype(bf16)
    third = (rest - second.astype(f32)).astype(bf16)
    k = lax.broadcasted_iota(jnp.int32, (pairs.shape[1], LANES), 0)
    j = lax.broadcasted_iota(jnp.int32, (pairs.shape[1], LANES), 1)

    def held(at):
        pick = (k == 256 * (j >> 5) + 32 * at + (j & 31)).astype(f32).astype(bf16)
        mine = dot(design, pick).astype(bf16)
        return dot(first, mine) + (dot(second, mine) + dot(third, mine))

    def keep(q, high_ref, low_ref):
        high, low = two(q[0:ND])
        high_ref[...] = jnp.concatenate([high, high], axis=1)
        low_ref[...] = low

    keep(held(z), q_high, q_low)

    @pl.when(next_to_end)
    def _():
        keep(jnp.where(at_z[:, 0:LANES] == end, 0.0, held(end)), e_high, e_low)


def kernel(
    ifg, pairs, out, x_buf, y_buf, p_buf, s_buf, fin, fr, ex, q_high, q_low, e_high, e_low,
    x_send, x_recv, y_send, y_recv, s_send, s_recv, f_send, f_recv, h_send, h_recv, go_line, go_all,
):
    stack = lax.axis_index("stack")
    slab = lax.axis_index("rows")
    slabs = lax.axis_size("rows")
    x = stack // (2 * LINE)
    z = (stack // 2) % LINE
    core = stack % 2
    me = 2 * x + core
    mirror = LINE - 1 - z
    half = z // (LINE // 2)
    near = z * (1 - half) + mirror * half
    end = (LINE - 1) * half
    at_end, next_to_end = near == 0, near == 1

    def peer(owner):
        return {"stack": 2 * LINE * (owner // 2) + 2 * z + owner % 2}

    def remote(src, dst, send, recv, device):
        return pltpu.make_async_remote_copy(
            src_ref=src, dst_ref=dst, send_sem=send, recv_sem=recv,
            device_id=device, device_id_type=pl.DeviceIdType.MESH,
        )

    def landed(ref, sem):
        pltpu.make_async_copy(ref, ref, sem).wait()

    def onward(way):
        return {"stack": stack + 2 - 4 * way}

    below = {"rows": slab + 1}
    above = {"rows": slab - 1}
    has_left, has_right = z > 0, z < LINE - 1
    has_above, has_below = slab > 0, slab < slabs - 1
    seam_below, seam_above = slab == slabs // 2 - 1, slab == slabs // 2
    gate_below, gate_above = seam_below & (z == LINE - 1), seam_above & (z == 0)
    gate_to_below = {"stack": stack - 2 * (LINE - 1), "rows": slab + 1}
    gate_to_above = {"stack": stack + 2 * (LINE - 1), "rows": slab - 1}

    barrier = pltpu.get_barrier_semaphore()

    def signal(sem, device):
        pl.semaphore_signal(sem, inc=1, device_id=device, device_id_type=pl.DeviceIdType.MESH)

    for step in range(1, OWNERS):
        signal(barrier, peer((me + step) % OWNERS))
    count = OWNERS - 1
    for there, device in (
        (has_left, onward(1)),
        (has_right, onward(0)),
        (has_above & jnp.logical_not(seam_above), above),
        (has_below & jnp.logical_not(seam_below), below),
        (gate_above, gate_to_above),
        (gate_below, gate_to_below),
    ):
        pl.when(there)(functools.partial(signal, barrier, device))
        count = count + there.astype(jnp.int32)
    pl.semaphore_wait(barrier, count)

    def band(c):
        return (c // 2 + BANDS - 1) % BANDS

    def half_rows(c):
        return pl.ds(HALF * (c % 2), HALF)

    def x_piece(c, owner):
        rows = pl.ds(8 * band(c) + HALF * (c % 2), HALF)
        return ifg.at[:, rows, pl.ds(pl.multiple_of(LANES * owner, LANES), LANES)]

    def x_slot(c):
        return x_buf.at[c // 2, pl.ds(DEPTH * me, DEPTH), half_rows(c)]

    def spread(c, carry):
        for step in range(1, OWNERS):
            owner = (me + step) % OWNERS
            remote(x_piece(c, owner), x_slot(c), x_send.at[c], x_recv.at[c], peer(owner)).start()
        pltpu.make_async_copy(x_piece(c, me), x_slot(c), x_recv.at[c]).start()
        return carry

    def x_landed(c):
        landed(x_buf.at[c // 2, :, half_rows(c)], x_recv.at[c])

    def whole(c, device):
        return remote(
            x_buf.at[c // 2, :, half_rows(c)], y_buf.at[c // 2, :, half_rows(c)], y_send.at[c], y_recv.at[c], device
        )

    lax.fori_loop(0, AHEAD, spread, 0)

    def spread_next(c):
        @pl.when(2 * c + AHEAD < CHUNKS)
        def _():
            spread(2 * c + AHEAD, 0)
            spread(2 * c + AHEAD + 1, 0)

    @pl.when(at_end)
    def _():
        def pass_on(c, carry):
            x_landed(c)
            whole(c, onward(half)).start()
            spread_next(c)
            return carry

        lax.fori_loop(0, WHOLE, pass_on, 0)

    tables(z, end, next_to_end, pairs, ex, q_high, q_low, e_high, e_low)

    @pl.when(jnp.logical_not(has_above))
    def _():
        fr[0] = jnp.zeros(fr.shape[1:], f32)

    @pl.when(jnp.logical_not(has_below))
    def _():
        fr[BANDS + 1] = jnp.zeros(fr.shape[1:], f32)

    taps = spatial_taps()

    def multiply(c, source, high_ref, low_ref, more):
        for s in range(0, HALF, 2):
            at = HALF * (c % 2) + s
            block = jnp.concatenate([source[c // 2, :, at], source[c // 2, :, at + 1]], axis=1)
            high, low = two(block)
            product = dot(high_ref[...], jnp.concatenate([high, low], axis=0)) + dot(low_ref[...], high)
            for t in range(2):
                part = product[:, LANES * t : LANES * (t + 1)].reshape(LINE, SHARE, LANES)
                p_buf[c, :, s + t] = part + p_buf[c, :, s + t] if more else part

    def compute(c):
        @pl.when(jnp.logical_not(at_end & (c < WHOLE)))
        def _():
            x_landed(c)
            spread_next(c)

        multiply(c, x_buf, q_high, q_low, False)

        @pl.when(next_to_end & (c < WHOLE))
        def _():
            landed(y_buf.at[c // 2, :, half_rows(c)], y_recv.at[c])
            multiply(c, y_buf, e_high, e_low, True)

    def low_pass(q):
        lane = lax.broadcasted_iota(jnp.int32, (8, LANES * OWNERS), 1)
        for i in range(KEEP):
            window = jnp.concatenate(
                [fr[q, :, i, 8 - R : 8], fr[q + 1, :, i], fr[q + 2, :, i, 0:R]], axis=1
            )
            rowpass = taps[R] * window[:, R : R + 8]
            for s in range(1, R + 1):
                rowpass = rowpass + taps[R + s] * (
                    window[:, R - s : R - s + 8] + window[:, R + s : R + s + 8]
                )
            line = jnp.concatenate([rowpass[o] for o in range(OWNERS)], axis=1)
            total = taps[R] * line
            width = LANES * OWNERS
            for s in range(1, R + 1):
                before = jnp.where(lane >= s, pltpu.roll(line, s, 1), 0.0)
                after = jnp.where(lane < width - s, pltpu.roll(line, width - s, 1), 0.0)
                total = total + taps[R + s] * (before + after)
            out[i, pl.ds(pl.multiple_of(8 * q, 8), 8)] = total

    halo_down = remote(
        fr.at[BANDS, :, :, pl.ds(8 - R, R)], fr.at[0, :, :, pl.ds(8 - R, R)], h_send.at[0], h_recv.at[0], below
    )
    halo_up = remote(
        fr.at[1, :, :, pl.ds(0, R)], fr.at[BANDS + 1, :, :, pl.ds(0, R)], h_send.at[1], h_recv.at[1], above
    )

    def finish(b):
        landed(fr.at[band(2 * b) + 1], f_recv.at[b])

        @pl.when((b == 0) & has_below & jnp.logical_not(seam_below))
        def _():
            halo_down.start()

        @pl.when((b == 1) & has_above & jnp.logical_not(seam_above))
        def _():
            halo_up.start()

        @pl.when((b == 2) & seam_below)
        def _():
            pl.when(has_right)(functools.partial(pl.semaphore_wait, go_all, 1))
            halo_down.start()

        @pl.when((b == 2) & seam_above)
        def _():
            pl.when(has_left)(functools.partial(pl.semaphore_wait, go_all, 1))
            halo_up.start()

        @pl.when(b >= 3)
        def _():
            low_pass(b - 2)

    def collect(c):
        for s in range(HALF):
            fin[c // 2, :, HALF * (c % 2) + s] = p_buf[c, z, s]

        @pl.when(c % 2 == 1)
        def _():
            b = c // 2
            slot = fr.at[band(c) + 1, me]
            for step in range(1, OWNERS):
                owner = (me + step) % OWNERS
                remote(fin.at[b, pl.ds(KEEP * owner, KEEP)], slot, f_send.at[b], f_recv.at[b], peer(owner)).start()
            pltpu.make_async_copy(fin.at[b, pl.ds(KEEP * me, KEEP)], slot, f_recv.at[b]).start()

            for gate, across, way in ((gate_below, gate_to_below, 1), (gate_above, gate_to_above, -1)):
                pl.when(gate & (b == 0))(functools.partial(signal, go_line, across))

                @pl.when(gate & (b == 1))
                def _():
                    pl.semaphore_wait(go_line, 1)
                    for hops in range(1, LINE):
                        signal(go_all, {"stack": stack - 2 * hops * way})

            @pl.when((b >= 1) & (b <= WHOLE // 2))
            def _():
                finish(b - 1)

    items = (LINE - 1) * CHUNKS
    first = (LINE - 1) * WHOLE

    def place(item):
        late = (item >= first).astype(jnp.int32)
        c = (item * 9363) >> 16
        after = item - first
        return (
            late * (WHOLE + (after & 7)) + (1 - late) * c,
            late * (after >> 3) + (1 - late) * (item - (LINE - 1) * c),
        )

    def flow(t, p, way, ends):
        item = t - LAG * p

        @pl.when((item >= 0) & (item < items))
        def _():
            c, hop = place(item)
            left_over = LINE - 1 - hop - p
            d = way * hop + (1 - way) * (LINE - 1 - hop)
            plain = c >= WHOLE

            @pl.when((ends == 0) & (hop == 0))
            def _():
                compute(c)

            @pl.when(left_over >= 0)
            def _():
                @pl.when((p > 1) | ((p == 1) & plain))
                def _():
                    landed(s_buf.at[way, c, d], s_recv.at[way, c, d])
                    p_buf[c, d] = p_buf[c, d] + s_buf[way, c, d]

                @pl.when((left_over > 0) & ((p > 0) | plain))
                def _():
                    remote(
                        p_buf.at[c, d], s_buf.at[way, c, d], s_send.at[way, c, d], s_recv.at[way, c, d], onward(way)
                    ).start()

                @pl.when((left_over == 0) & ((jnp.logical_not(plain) | at_end) if ends else plain))
                def _():
                    collect(c)

    def step(t, carry):
        flow(t, near, half, 0)
        flow(t, LINE - 1 - near, 1 - half, 1)
        return carry

    steps = max(items + LAG, first + CHUNKS - WHOLE + (LINE - 1) * LAG)
    lax.fori_loop(0, steps, step, 0)

    def rest(b, carry):
        finish(b)
        return carry

    lax.fori_loop(WHOLE // 2, BANDS, rest, 0)

    @pl.when(has_above)
    def _():
        halo_down.wait_recv()
        halo_up.wait_send()

    @pl.when(has_below)
    def _():
        halo_up.wait_recv()
        halo_down.wait_send()

    def tail(q, carry):
        low_pass(q)
        return carry

    low_pass(0)
    lax.fori_loop(BANDS - 2, BANDS, tail, 0)

    def drain(c, carry):
        landed(x_buf.at[0, pl.ds(0, (OWNERS - 1) * DEPTH), pl.ds(0, HALF)], x_send.at[c])
        head = at_end & (c < WHOLE)

        @pl.when(head)
        def _():
            landed(x_buf.at[0, :, pl.ds(0, HALF)], y_send.at[c])

        def each(d, carry):
            @pl.when((d > z) & jnp.logical_not((z == 0) & head))
            def _():
                landed(p_buf.at[c, d], s_send.at[0, c, d])

            @pl.when((d < z) & jnp.logical_not((mirror == 0) & head))
            def _():
                landed(p_buf.at[c, d], s_send.at[1, c, d])

            return carry

        return lax.fori_loop(0, LINE, each, carry)

    lax.fori_loop(0, CHUNKS, drain, 0)

    def drain_bands(b, carry):
        landed(fr.at[1, pl.ds(0, OWNERS - 1)], f_send.at[b])
        return carry

    lax.fori_loop(0, BANDS, drain_bands, 0)


def shards(interferograms, pairs):
    dma = pltpu.SemaphoreType.DMA
    block = (CHUNKS, LINE, HALF, SHARE, LANES)
    held = (BANDS, DEPTH * OWNERS, 8, LANES)
    return pl.pallas_call(
        kernel,
        out_shape=jax.ShapeDtypeStruct((KEEP,) + interferograms.shape[1:], f32),
        in_specs=[pl.BlockSpec(memory_space=pltpu.HBM), pl.BlockSpec(memory_space=pltpu.VMEM)],
        out_specs=pl.BlockSpec(memory_space=pltpu.VMEM),
        scratch_shapes=[
            pltpu.VMEM(held, f32),
            pltpu.VMEM((WHOLE // 2,) + held[1:], f32),
            pltpu.VMEM(block, f32),
            pltpu.VMEM((2,) + block, f32),
            pltpu.VMEM((BANDS, SHARE, 8, LANES), f32),
            pltpu.VMEM((BANDS + 2, OWNERS, KEEP, 8, LANES), f32),
            pltpu.VMEM((2 * PAD, PAD), f32),
            pltpu.VMEM((ND, 2 * LANES), bf16),
            pltpu.VMEM((ND, LANES), bf16),
            pltpu.VMEM((ND, 2 * LANES), bf16),
            pltpu.VMEM((ND, LANES), bf16),
            dma((CHUNKS,)), dma((CHUNKS,)),
            dma((WHOLE,)), dma((WHOLE,)),
            dma((2, CHUNKS, LINE)), dma((2, CHUNKS, LINE)),
            dma((BANDS,)), dma((BANDS,)),
            dma((2,)), dma((2,)),
            pltpu.SemaphoreType.REGULAR, pltpu.SemaphoreType.REGULAR,
        ],
        compiler_params=pltpu.CompilerParams(
            collective_id=0, has_side_effects=True, vmem_limit_bytes=61 * 1024 * 1024
        ),
    )(interferograms, pairs.T)


def solution(mesh):
    return jax.shard_map(
        shards,
        mesh=mesh,
        in_specs=(P("stack", "rows", None), P()),
        out_specs=P("stack", "rows", None),
        check_vma=False,
    )
```

```python
import functools

import jax
import jax.numpy as jnp
import numpy as np
from jax import lax
from jax.experimental import pallas as pl
from jax.experimental.pallas import tpu as pltpu
from jax.sharding import PartitionSpec as P

ND = 192
R = 4
TIKHONOV = 0.1
TEMPORAL_SIGMA = 6.0
SPATIAL_SIGMA = 1.5

LINE = 8
OWNERS = 8
DEPTH = 16
LANES = 128
BANDS = 8
CHUNKS = 16
HALF = 4
SHARE = ND // LINE
KEEP = ND // (LINE * OWNERS)
PAD = 256
WHOLE = 8
LAG = 6
AHEAD = 4
DIRECT = 2
ROUNDS = 9
f32 = jnp.float32
bf16 = jnp.bfloat16


def spatial_taps():
    offsets = np.arange(-R, R + 1).astype(np.float32) / np.float32(SPATIAL_SIGMA)
    taps = np.exp(np.float32(-0.5) * offsets * offsets)
    return [float(tap) for tap in (taps / np.sum(taps)).astype(np.float32)]


def dot(a, b):
    return jnp.dot(a, b, preferred_element_type=f32)


def two(a):
    high = a.astype(bf16)
    return high, (a - high.astype(f32)).astype(bf16)


def dot3(a, b):
    ah, al = two(a)
    bh, bl = two(b)
    return dot(ah, bh) + (dot(ah, bl) + dot(al, bh))


def dot6(a, b):
    return jnp.dot(a, b, precision=lax.Precision.HIGHEST, preferred_element_type=f32)


def inverse(normal, eye, ex):
    top = jnp.max(jnp.sum(jnp.abs(normal), axis=1, keepdims=True), axis=0, keepdims=True)
    scale = 2.0 / (top + TIKHONOV)
    ex[0:PAD] = eye - scale * normal
    ex[PAD : 2 * PAD] = scale * eye

    def turn(_, rho):
        both = ex[...]
        err = both[0:PAD]
        product = dot3(both, err)
        gain = 2.0 / (2.0 - rho * rho)
        ex[0:PAD] = gain * product[0:PAD] + (1.0 - gain) * eye
        ex[PAD : 2 * PAD] = gain * (both[PAD : 2 * PAD] + product[PAD : 2 * PAD])
        return 0.5 * rho * rho * gain

    lax.fori_loop(0, ROUNDS, turn, (top - TIKHONOV) / (top + TIKHONOV))

    def polish(_, carry):
        now = ex[PAD : 2 * PAD]
        left = eye - dot6(normal, now)
        ex[PAD : 2 * PAD] = now + dot3(now, left)
        return carry

    lax.fori_loop(0, 3, polish, 0)
    return ex[PAD : 2 * PAD]


def tables(z, end, next_to_end, pairs, ex, q_high, q_low, e_high, e_low):
    dates = lax.broadcasted_iota(jnp.int32, (PAD, pairs.shape[1]), 0)
    design = (dates == pairs[1:2, :]).astype(f32) - (dates == pairs[0:1, :]).astype(f32)
    design = design.astype(bf16)
    row = lax.broadcasted_iota(jnp.int32, (PAD, PAD), 0)
    col = lax.broadcasted_iota(jnp.int32, (PAD, PAD), 1)
    eye = (row == col).astype(f32)
    normal = lax.dot_general(design, design, (((1,), (1,)), ((), ())), preferred_element_type=f32)
    normal = normal + TIKHONOV * eye
    solved = inverse(normal, eye, ex)
    at_z = (row * 2731) >> 16
    rest = row - SHARE * at_z
    at_x = (rest * 43) >> 8
    date = 48 * at_x + 6 * at_z + (rest - 6 * at_x)
    offset = (date - col).astype(f32) / TEMPORAL_SIGMA
    weight = jnp.where(col < ND, jnp.exp(-0.5 * offset * offset), 0.0)
    smooth = weight / jnp.sum(weight, axis=1, keepdims=True)
    change = dot6((date == col).astype(f32) - smooth, solved)
    first = change.astype(bf16)
    rest = change - first.astype(f32)
    second = rest.astype(bf16)
    third = (rest - second.astype(f32)).astype(bf16)
    k = lax.broadcasted_iota(jnp.int32, (pairs.shape[1], LANES), 0)
    j = lax.broadcasted_iota(jnp.int32, (pairs.shape[1], LANES), 1)

    def held(at):
        pick = (k == 256 * (j >> 5) + 32 * at + (j & 31)).astype(f32).astype(bf16)
        mine = dot(design, pick).astype(bf16)
        return dot(first, mine) + (dot(second, mine) + dot(third, mine))

    def keep(q, high_ref, low_ref):
        high, low = two(q[0:ND])
        high_ref[...] = jnp.concatenate([high, high], axis=1)
        low_ref[...] = low

    keep(held(z), q_high, q_low)

    @pl.when(next_to_end)
    def _():
        keep(jnp.where(at_z[:, 0:LANES] == end, 0.0, held(end)), e_high, e_low)


def kernel(
    ifg, pairs, out, x_buf, y_buf, p_buf, s_buf, fin, fr, ex, q_high, q_low, e_high, e_low,
    x_send, x_recv, y_send, y_recv, s_send, s_recv, f_send, f_recv, h_send, h_recv, go_line, go_all,
):
    stack = lax.axis_index("stack")
    slab = lax.axis_index("rows")
    slabs = lax.axis_size("rows")
    x = stack // (2 * LINE)
    z = (stack // 2) % LINE
    core = stack % 2
    me = 2 * x + core
    mirror = LINE - 1 - z
    half = z // (LINE // 2)
    near = z * (1 - half) + mirror * half
    end = (LINE - 1) * half
    at_end, next_to_end = near == 0, near == 1

    def peer(owner):
        return {"stack": 2 * LINE * (owner // 2) + 2 * z + owner % 2}

    def remote(src, dst, send, recv, device):
        return pltpu.make_async_remote_copy(
            src_ref=src, dst_ref=dst, send_sem=send, recv_sem=recv,
            device_id=device, device_id_type=pl.DeviceIdType.MESH,
        )

    def landed(ref, sem):
        pltpu.make_async_copy(ref, ref, sem).wait()

    def onward(way):
        return {"stack": stack + 2 - 4 * way}

    below = {"rows": slab + 1}
    above = {"rows": slab - 1}
    has_left, has_right = z > 0, z < LINE - 1
    has_above, has_below = slab > 0, slab < slabs - 1
    seam_below, seam_above = slab == slabs // 2 - 1, slab == slabs // 2
    gate_below, gate_above = seam_below & (z == LINE - 1), seam_above & (z == 0)
    gate_to_below = {"stack": stack - 2 * (LINE - 1), "rows": slab + 1}
    gate_to_above = {"stack": stack + 2 * (LINE - 1), "rows": slab - 1}

    barrier = pltpu.get_barrier_semaphore()

    def signal(sem, device):
        pl.semaphore_signal(sem, inc=1, device_id=device, device_id_type=pl.DeviceIdType.MESH)

    def beside(owner, way):
        return {"stack": 2 * LINE * (owner // 2) + 2 * (z + 1 - 2 * way) + owner % 2}

    for step in range(1, OWNERS):
        signal(barrier, peer((me + step) % OWNERS))
    count = OWNERS - 1
    ends_pair = at_end | next_to_end
    pair_way = half * at_end.astype(jnp.int32) + (1 - half) * next_to_end.astype(jnp.int32)

    @pl.when(ends_pair)
    def _():
        for step in range(1, OWNERS):
            signal(barrier, beside((me + step) % OWNERS, pair_way))

    count = count + (OWNERS - 1) * ends_pair.astype(jnp.int32)
    for there, device in (
        (has_left, onward(1)),
        (has_right, onward(0)),
        (has_above & jnp.logical_not(seam_above), above),
        (has_below & jnp.logical_not(seam_below), below),
        (gate_above, gate_to_above),
        (gate_below, gate_to_below),
    ):
        pl.when(there)(functools.partial(signal, barrier, device))
        count = count + there.astype(jnp.int32)
    pl.semaphore_wait(barrier, count)

    def band(c):
        return (c // 2 + BANDS - 1) % BANDS

    def half_rows(c):
        return pl.ds(HALF * (c % 2), HALF)

    def x_piece(c, owner):
        rows = pl.ds(8 * band(c) + HALF * (c % 2), HALF)
        return ifg.at[:, rows, pl.ds(pl.multiple_of(LANES * owner, LANES), LANES)]

    def x_slot(c):
        return x_buf.at[c // 2, pl.ds(DEPTH * me, DEPTH), half_rows(c)]

    def spread(c, carry):
        for step in range(1, OWNERS):
            owner = (me + step) % OWNERS
            remote(x_piece(c, owner), x_slot(c), x_send, x_recv.at[c], peer(owner)).start()
        pltpu.make_async_copy(x_piece(c, me), x_slot(c), x_recv.at[c]).start()
        return carry

    def x_landed(c):
        landed(x_buf.at[c // 2, :, half_rows(c)], x_recv.at[c])

    def whole(c, device):
        return remote(
            x_buf.at[c // 2, :, half_rows(c)], y_buf.at[c // 2, :, half_rows(c)], y_send, y_recv.at[c], device
        )

    def spread_direct(c, carry):
        for step in range(OWNERS):
            owner = (me + step) % OWNERS
            slot = y_buf.at[c // 2, pl.ds(DEPTH * me, DEPTH), half_rows(c)]
            remote(x_piece(c, owner), slot, y_send, y_recv.at[c], beside(owner, half)).start()
        return carry

    @pl.when(at_end)
    def _():
        lax.fori_loop(0, DIRECT, spread_direct, 0)

    lax.fori_loop(0, AHEAD, spread, 0)

    def spread_next(c):
        @pl.when(2 * c + AHEAD < CHUNKS)
        def _():
            spread(2 * c + AHEAD, 0)
            spread(2 * c + AHEAD + 1, 0)

    @pl.when(at_end)
    def _():
        def pass_on(c, carry):
            x_landed(c)

            @pl.when(c >= DIRECT)
            def _():
                whole(c, onward(half)).start()

            spread_next(c)
            return carry

        lax.fori_loop(0, WHOLE, pass_on, 0)

    tables(z, end, next_to_end, pairs, ex, q_high, q_low, e_high, e_low)

    @pl.when(jnp.logical_not(has_above))
    def _():
        fr[0] = jnp.zeros(fr.shape[1:], f32)

    @pl.when(jnp.logical_not(has_below))
    def _():
        fr[BANDS + 1] = jnp.zeros(fr.shape[1:], f32)

    taps = spatial_taps()

    def multiply(c, source, high_ref, low_ref, more):
        for s in range(0, HALF, 2):
            at = HALF * (c % 2) + s
            block = jnp.concatenate([source[c // 2, :, at], source[c // 2, :, at + 1]], axis=1)
            high, low = two(block)
            product = dot(high_ref[...], jnp.concatenate([high, low], axis=0)) + dot(low_ref[...], high)
            for t in range(2):
                part = product[:, LANES * t : LANES * (t + 1)].reshape(LINE, SHARE, LANES)
                p_buf[c, :, s + t] = part + p_buf[c, :, s + t] if more else part

    def compute(c):
        @pl.when(jnp.logical_not(at_end & (c < WHOLE)))
        def _():
            x_landed(c)
            spread_next(c)

        multiply(c, x_buf, q_high, q_low, False)

        @pl.when(next_to_end & (c < WHOLE))
        def _():
            landed(y_buf.at[c // 2, :, half_rows(c)], y_recv.at[c])
            multiply(c, y_buf, e_high, e_low, True)

    def low_pass(q):
        lane = lax.broadcasted_iota(jnp.int32, (8, LANES * OWNERS), 1)
        for i in range(KEEP):
            window = jnp.concatenate(
                [fr[q, :, i, 8 - R : 8], fr[q + 1, :, i], fr[q + 2, :, i, 0:R]], axis=1
            )
            rowpass = taps[R] * window[:, R : R + 8]
            for s in range(1, R + 1):
                rowpass = rowpass + taps[R + s] * (
                    window[:, R - s : R - s + 8] + window[:, R + s : R + s + 8]
                )
            line = jnp.concatenate([rowpass[o] for o in range(OWNERS)], axis=1)
            total = taps[R] * line
            width = LANES * OWNERS
            for s in range(1, R + 1):
                before = jnp.where(lane >= s, pltpu.roll(line, s, 1), 0.0)
                after = jnp.where(lane < width - s, pltpu.roll(line, width - s, 1), 0.0)
                total = total + taps[R + s] * (before + after)
            out[i, pl.ds(pl.multiple_of(8 * q, 8), 8)] = total

    halo_down = remote(
        fr.at[BANDS, :, :, pl.ds(8 - R, R)], fr.at[0, :, :, pl.ds(8 - R, R)], h_send.at[0], h_recv.at[0], below
    )
    halo_up = remote(
        fr.at[1, :, :, pl.ds(0, R)], fr.at[BANDS + 1, :, :, pl.ds(0, R)], h_send.at[1], h_recv.at[1], above
    )

    def finish(b):
        landed(fr.at[band(2 * b) + 1], f_recv.at[b])

        @pl.when((b == 0) & has_below & jnp.logical_not(seam_below))
        def _():
            halo_down.start()

        @pl.when((b == 1) & has_above & jnp.logical_not(seam_above))
        def _():
            halo_up.start()

        @pl.when((b == 2) & seam_below)
        def _():
            pl.when(has_right)(functools.partial(pl.semaphore_wait, go_all, 1))
            halo_down.start()

        @pl.when((b == 2) & seam_above)
        def _():
            pl.when(has_left)(functools.partial(pl.semaphore_wait, go_all, 1))
            halo_up.start()

        @pl.when(b >= 3)
        def _():
            low_pass(b - 2)

    def collect(c):
        for s in range(HALF):
            fin[c // 2, :, HALF * (c % 2) + s] = p_buf[c, z, s]

        @pl.when(c % 2 == 1)
        def _():
            b = c // 2
            slot = fr.at[band(c) + 1, me]
            for step in range(1, OWNERS):
                owner = (me + step) % OWNERS
                remote(fin.at[b, pl.ds(KEEP * owner, KEEP)], slot, f_send, f_recv.at[b], peer(owner)).start()
            pltpu.make_async_copy(fin.at[b, pl.ds(KEEP * me, KEEP)], slot, f_recv.at[b]).start()

            for gate, across, way in ((gate_below, gate_to_below, 1), (gate_above, gate_to_above, -1)):
                pl.when(gate & (b == 0))(functools.partial(signal, go_line, across))

                @pl.when(gate & (b == 1))
                def _():
                    pl.semaphore_wait(go_line, 1)
                    for hops in range(1, LINE):
                        signal(go_all, {"stack": stack - 2 * hops * way})

            @pl.when((b >= 1) & (b <= WHOLE // 2))
            def _():
                finish(b - 1)

    items = (LINE - 1) * CHUNKS
    first = (LINE - 1) * WHOLE

    def place(item):
        late = (item >= first).astype(jnp.int32)
        c = (item * 9363) >> 16
        after = item - first
        return (
            late * (WHOLE + (after & 7)) + (1 - late) * c,
            late * (after >> 3) + (1 - late) * (item - (LINE - 1) * c),
        )

    def flow(t, p, way, ends):
        item = t - LAG * p

        @pl.when((item >= 0) & (item < items))
        def _():
            c, hop = place(item)
            left_over = LINE - 1 - hop - p
            d = way * hop + (1 - way) * (LINE - 1 - hop)
            plain = c >= WHOLE

            @pl.when((ends == 0) & (hop == 0))
            def _():
                compute(c)

            @pl.when(left_over >= 0)
            def _():
                @pl.when((p > 1) | ((p == 1) & plain))
                def _():
                    landed(s_buf.at[way, c, d], s_recv.at[way, c, hop])
                    p_buf[c, d] = p_buf[c, d] + s_buf[way, c, d]

                @pl.when((left_over > 0) & ((p > 0) | plain))
                def _():
                    remote(
                        p_buf.at[c, d], s_buf.at[way, c, d], s_send.at[way], s_recv.at[way, c, hop], onward(way)
                    ).start()

                @pl.when((left_over == 0) & ((jnp.logical_not(plain) | at_end) if ends else plain))
                def _():
                    collect(c)

    def step(t, carry):
        flow(t, near, half, 0)
        flow(t, LINE - 1 - near, 1 - half, 1)
        return carry

    steps = max(items + LAG, first + CHUNKS - WHOLE + (LINE - 1) * LAG)
    lax.fori_loop(0, steps, step, 0)

    def rest(b, carry):
        finish(b)
        return carry

    lax.fori_loop(WHOLE // 2, BANDS, rest, 0)

    @pl.when(has_above)
    def _():
        halo_down.wait_recv()
        halo_up.wait_send()

    @pl.when(has_below)
    def _():
        halo_up.wait_recv()
        halo_down.wait_send()

    def tail(q, carry):
        low_pass(q)
        return carry

    low_pass(0)
    lax.fori_loop(BANDS - 2, BANDS, tail, 0)

    landed(x_buf.at[:, pl.ds(0, (OWNERS - 1) * DEPTH)], x_send)
    landed(fr.at[pl.ds(1, BANDS), pl.ds(0, OWNERS - 1)], f_send)
    pl.when(at_end)(functools.partial(landed, y_buf, y_send))
    for way, p in ((0, z), (1, mirror)):
        for k in range(LINE - 1):
            chunks = pl.ds(0, CHUNKS) if k else pl.ds(WHOLE, CHUNKS - WHOLE)
            ahead = p_buf.at[chunks, pl.ds(0, LINE - 1 - k)]
            pl.when(p == k)(functools.partial(landed, ahead, s_send.at[way]))


def shards(interferograms, pairs):
    dma = pltpu.SemaphoreType.DMA
    block = (CHUNKS, LINE, HALF, SHARE, LANES)
    held = (BANDS, DEPTH * OWNERS, 8, LANES)
    return pl.pallas_call(
        kernel,
        out_shape=pltpu.VMEM((KEEP,) + interferograms.shape[1:], f32),
        in_specs=[pl.BlockSpec(memory_space=pltpu.HBM), pl.BlockSpec(memory_space=pltpu.VMEM)],
        out_specs=pl.BlockSpec(memory_space=pltpu.VMEM),
        scratch_shapes=[
            pltpu.VMEM(held, f32),
            pltpu.VMEM((WHOLE // 2,) + held[1:], f32),
            pltpu.VMEM(block, f32),
            pltpu.VMEM((2,) + block, f32),
            pltpu.VMEM((BANDS, SHARE, 8, LANES), f32),
            pltpu.VMEM((BANDS + 2, OWNERS, KEEP, 8, LANES), f32),
            pltpu.VMEM((2 * PAD, PAD), f32),
            pltpu.VMEM((ND, 2 * LANES), bf16),
            pltpu.VMEM((ND, LANES), bf16),
            pltpu.VMEM((ND, 2 * LANES), bf16),
            pltpu.VMEM((ND, LANES), bf16),
            dma, dma((CHUNKS,)),
            dma, dma((WHOLE,)),
            dma((2,)), dma((2, CHUNKS, LINE - 1)),
            dma, dma((BANDS,)),
            dma((2,)), dma((2,)),
            pltpu.SemaphoreType.REGULAR, pltpu.SemaphoreType.REGULAR,
        ],
        compiler_params=pltpu.CompilerParams(
            collective_id=0, has_side_effects=True, vmem_limit_bytes=61 * 1024 * 1024
        ),
    )(interferograms, pairs.T)


def solution(mesh):
    return jax.shard_map(
        shards,
        mesh=mesh,
        in_specs=(P("stack", "rows", None), P()),
        out_specs=P("stack", "rows", None),
        check_vma=False,
    )
```

```python
import functools

import jax
import jax.numpy as jnp
import numpy as np
from jax import lax
from jax.experimental import pallas as pl
from jax.experimental.pallas import tpu as pltpu
from jax.sharding import PartitionSpec as P

ND = 192
R = 4
TIKHONOV = 0.1
TEMPORAL_SIGMA = 6.0
SPATIAL_SIGMA = 1.5

LINE = 8
OWNERS = 8
DEPTH = 16
LANES = 128
BANDS = 8
CHUNKS = 16
HALF = 4
UNITS = 9
SHARE = ND // LINE
KEEP = ND // (LINE * OWNERS)
PAD = 256
WHOLE = 8
LAG = 6
AHEAD = 4
DIRECT = 2
ROUNDS = 9
f32 = jnp.float32
bf16 = jnp.bfloat16


def spatial_taps():
    offsets = np.arange(-R, R + 1).astype(np.float32) / np.float32(SPATIAL_SIGMA)
    taps = np.exp(np.float32(-0.5) * offsets * offsets)
    return [float(tap) for tap in (taps / np.sum(taps)).astype(np.float32)]


def dot(a, b):
    return jnp.dot(a, b, preferred_element_type=f32)


def two(a):
    high = a.astype(bf16)
    return high, (a - high.astype(f32)).astype(bf16)


def dot3(a, b):
    ah, al = two(a)
    bh, bl = two(b)
    return dot(ah, bh) + (dot(ah, bl) + dot(al, bh))


def dot6(a, b):
    return jnp.dot(a, b, precision=lax.Precision.HIGHEST, preferred_element_type=f32)


def inverse(normal, eye, ex):
    top = jnp.max(jnp.sum(jnp.abs(normal), axis=1, keepdims=True), axis=0, keepdims=True)
    scale = 2.0 / (top + TIKHONOV)
    ex[0:PAD] = eye - scale * normal
    ex[PAD : 2 * PAD] = scale * eye

    def turn(_, rho):
        both = ex[...]
        err = both[0:PAD]
        product = dot3(both, err)
        gain = 2.0 / (2.0 - rho * rho)
        ex[0:PAD] = gain * product[0:PAD] + (1.0 - gain) * eye
        ex[PAD : 2 * PAD] = gain * (both[PAD : 2 * PAD] + product[PAD : 2 * PAD])
        return 0.5 * rho * rho * gain

    lax.fori_loop(0, ROUNDS, turn, (top - TIKHONOV) / (top + TIKHONOV))

    def polish(_, carry):
        now = ex[PAD : 2 * PAD]
        left = eye - dot6(normal, now)
        ex[PAD : 2 * PAD] = now + dot3(now, left)
        return carry

    lax.fori_loop(0, 3, polish, 0)
    return ex[PAD : 2 * PAD]


def network(pairs):
    dates = lax.broadcasted_iota(jnp.int32, (PAD, pairs.shape[1]), 0)
    design = (dates == pairs[1:2, :]).astype(f32) - (dates == pairs[0:1, :]).astype(f32)
    design = design.astype(bf16)
    return design, lax.dot_general(design, design, (((1,), (1,)), ((), ())), preferred_element_type=f32)


def tables(z, end, next_to_end, pairs, design_ref, ex, q_high, q_low, e_high, e_low):
    design = design_ref[...]
    row = lax.broadcasted_iota(jnp.int32, (PAD, PAD), 0)
    col = lax.broadcasted_iota(jnp.int32, (PAD, PAD), 1)
    eye = (row == col).astype(f32)
    normal = ex[0:PAD] + TIKHONOV * eye
    solved = inverse(normal, eye, ex)
    at_z = (row * 2731) >> 16
    rest = row - SHARE * at_z
    at_x = (rest * 43) >> 8
    date = 48 * at_x + 6 * at_z + (rest - 6 * at_x)
    offset = (date - col).astype(f32) / TEMPORAL_SIGMA
    weight = jnp.where(col < ND, jnp.exp(-0.5 * offset * offset), 0.0)
    smooth = weight / jnp.sum(weight, axis=1, keepdims=True)
    change = dot6((date == col).astype(f32) - smooth, solved)
    first = change.astype(bf16)
    rest = change - first.astype(f32)
    second = rest.astype(bf16)
    third = (rest - second.astype(f32)).astype(bf16)
    k = lax.broadcasted_iota(jnp.int32, (pairs.shape[1], LANES), 0)
    j = lax.broadcasted_iota(jnp.int32, (pairs.shape[1], LANES), 1)

    def held(at):
        pick = (k == 256 * (j >> 5) + 32 * at + (j & 31)).astype(f32).astype(bf16)
        mine = dot(design, pick).astype(bf16)
        return dot(first, mine) + (dot(second, mine) + dot(third, mine))

    def keep(q, high_ref, low_ref):
        high, low = two(q[0:ND])
        high_ref[...] = jnp.concatenate([high, high], axis=1)
        low_ref[...] = low

    keep(held(z), q_high, q_low)

    @pl.when(next_to_end)
    def _():
        keep(jnp.where(at_z[:, 0:LANES] == end, 0.0, held(end)), e_high, e_low)


def kernel(
    ifg, pairs, out, x_buf, y_buf, p_buf, s_buf, fin, fr, design_ref, ex, q_high, q_low, e_high, e_low,
    x_send, x_recv, y_send, y_recv, s_send, s_recv, f_send, f_recv, h_send, h_recv, go_line, go_all,
):
    stack = lax.axis_index("stack")
    slab = lax.axis_index("rows")
    slabs = lax.axis_size("rows")
    x = stack // (2 * LINE)
    z = (stack // 2) % LINE
    core = stack % 2
    me = 2 * x + core
    mirror = LINE - 1 - z
    half = z // (LINE // 2)
    near = z * (1 - half) + mirror * half
    end = (LINE - 1) * half
    at_end, next_to_end = near == 0, near == 1

    def peer(owner):
        return {"stack": 2 * LINE * (owner // 2) + 2 * z + owner % 2}

    def remote(src, dst, send, recv, device):
        return pltpu.make_async_remote_copy(
            src_ref=src, dst_ref=dst, send_sem=send, recv_sem=recv,
            device_id=device, device_id_type=pl.DeviceIdType.MESH,
        )

    def landed(ref, sem):
        pltpu.make_async_copy(ref, ref, sem).wait()

    def onward(way):
        return {"stack": stack + 2 - 4 * way}

    below = {"rows": slab + 1}
    above = {"rows": slab - 1}
    has_left, has_right = z > 0, z < LINE - 1
    has_above, has_below = slab > 0, slab < slabs - 1
    seam_below, seam_above = slab == slabs // 2 - 1, slab == slabs // 2
    gate_below, gate_above = seam_below & (z == LINE - 1), seam_above & (z == 0)
    gate_to_below = {"stack": stack - 2 * (LINE - 1), "rows": slab + 1}
    gate_to_above = {"stack": stack + 2 * (LINE - 1), "rows": slab - 1}

    barrier = pltpu.get_barrier_semaphore()

    def signal(sem, device):
        pl.semaphore_signal(sem, inc=1, device_id=device, device_id_type=pl.DeviceIdType.MESH)

    def beside(owner, way):
        return {"stack": 2 * LINE * (owner // 2) + 2 * (z + 1 - 2 * way) + owner % 2}

    for step in range(1, OWNERS):
        signal(barrier, peer((me + step) % OWNERS))
    count = OWNERS - 1
    ends_pair = at_end | next_to_end
    pair_way = half * at_end.astype(jnp.int32) + (1 - half) * next_to_end.astype(jnp.int32)

    @pl.when(ends_pair)
    def _():
        for step in range(1, OWNERS):
            signal(barrier, beside((me + step) % OWNERS, pair_way))

    count = count + (OWNERS - 1) * ends_pair.astype(jnp.int32)
    for there, device in (
        (has_left, onward(1)),
        (has_right, onward(0)),
        (has_above & jnp.logical_not(seam_above), above),
        (has_below & jnp.logical_not(seam_below), below),
        (gate_above, gate_to_above),
        (gate_below, gate_to_below),
    ):
        pl.when(there)(functools.partial(signal, barrier, device))
        count = count + there.astype(jnp.int32)
    design_ref[...], ex[0:PAD] = network(pairs)
    pl.semaphore_wait(barrier, count)

    def band(c):
        return (c // 2 + BANDS - 1) % BANDS

    def half_rows(c):
        return pl.ds(HALF * (c % 2), HALF)

    def x_piece(c, owner):
        rows = pl.ds(8 * band(c) + HALF * (c % 2), HALF)
        return ifg.at[:, rows, pl.ds(pl.multiple_of(LANES * owner, LANES), LANES)]

    def x_slot(c):
        return x_buf.at[c // 2, pl.ds(DEPTH * me, DEPTH), half_rows(c)]

    def spread(c, carry):
        for step in range(1, OWNERS):
            owner = (me + step) % OWNERS
            remote(x_piece(c, owner), x_slot(c), x_send, x_recv.at[c], peer(owner)).start()
        pltpu.make_async_copy(x_piece(c, me), x_slot(c), x_recv.at[c]).start()
        return carry

    def x_landed(c):
        landed(x_buf.at[c // 2, :, half_rows(c)], x_recv.at[c])

    def whole(c, device):
        return remote(
            x_buf.at[c // 2, :, half_rows(c)], y_buf.at[c // 2, :, half_rows(c)], y_send, y_recv.at[c + 1], device
        )

    def spread_direct(unit, band_row, height):
        for step in range(OWNERS):
            owner = (me + step) % OWNERS
            piece = ifg.at[
                :, pl.ds(8 * band(0) + band_row, height), pl.ds(pl.multiple_of(LANES * owner, LANES), LANES)
            ]
            slot = y_buf.at[0, pl.ds(DEPTH * me, DEPTH), pl.ds(band_row, height)]
            remote(piece, slot, y_send, y_recv.at[unit], beside(owner, half)).start()

    @pl.when(at_end)
    def _():
        spread_direct(0, 0, HALF // 2)
        spread_direct(1, HALF // 2, HALF // 2)
        spread_direct(2, HALF, HALF)

    lax.fori_loop(0, AHEAD, spread, 0)

    def spread_next(c):
        @pl.when(2 * c + AHEAD < CHUNKS)
        def _():
            spread(2 * c + AHEAD, 0)
            spread(2 * c + AHEAD + 1, 0)

    @pl.when(at_end)
    def _():
        def pass_on(c, carry):
            x_landed(c)

            @pl.when(c >= DIRECT)
            def _():
                whole(c, onward(half)).start()

            spread_next(c)
            return carry

        lax.fori_loop(0, WHOLE, pass_on, 0)

    tables(z, end, next_to_end, pairs, design_ref, ex, q_high, q_low, e_high, e_low)

    @pl.when(jnp.logical_not(has_above))
    def _():
        fr[0] = jnp.zeros(fr.shape[1:], f32)

    @pl.when(jnp.logical_not(has_below))
    def _():
        fr[BANDS + 1] = jnp.zeros(fr.shape[1:], f32)

    taps = spatial_taps()

    def multiply(c, source, high_ref, low_ref, more, rows=range(0, HALF, 2)):
        for s in rows:
            at = HALF * (c % 2) + s
            block = jnp.concatenate([source[c // 2, :, at], source[c // 2, :, at + 1]], axis=1)
            high, low = two(block)
            product = dot(high_ref[...], jnp.concatenate([high, low], axis=0)) + dot(low_ref[...], high)
            for t in range(2):
                part = product[:, LANES * t : LANES * (t + 1)].reshape(LINE, SHARE, LANES)
                p_buf[c, :, s + t] = part + p_buf[c, :, s + t] if more else part

    def compute(c):
        @pl.when(jnp.logical_not(at_end & (c < WHOLE)))
        def _():
            x_landed(c)
            spread_next(c)

        multiply(c, x_buf, q_high, q_low, False)

    def compute_end(c):
        landed(y_buf.at[c // 2, :, half_rows(c)], y_recv.at[c + 1])
        multiply(c, y_buf, e_high, e_low, True)

    def compute_part(unit):
        landed(y_buf.at[0, :, pl.ds(HALF // 2 * unit, HALF // 2)], y_recv.at[unit])
        multiply(0, y_buf, e_high, e_low, True, (HALF // 2 * unit,))

    def low_pass(q):
        lane = lax.broadcasted_iota(jnp.int32, (8, LANES * OWNERS), 1)
        for i in range(KEEP):
            window = jnp.concatenate(
                [fr[q, :, i, 8 - R : 8], fr[q + 1, :, i], fr[q + 2, :, i, 0:R]], axis=1
            )
            rowpass = taps[R] * window[:, R : R + 8]
            for s in range(1, R + 1):
                rowpass = rowpass + taps[R + s] * (
                    window[:, R - s : R - s + 8] + window[:, R + s : R + s + 8]
                )
            line = jnp.concatenate([rowpass[o] for o in range(OWNERS)], axis=1)
            total = taps[R] * line
            width = LANES * OWNERS
            for s in range(1, R + 1):
                before = jnp.where(lane >= s, pltpu.roll(line, s, 1), 0.0)
                after = jnp.where(lane < width - s, pltpu.roll(line, width - s, 1), 0.0)
                total = total + taps[R + s] * (before + after)
            out[i, pl.ds(pl.multiple_of(8 * q, 8), 8)] = total

    halo_down = remote(
        fr.at[BANDS, :, :, pl.ds(8 - R, R)], fr.at[0, :, :, pl.ds(8 - R, R)], h_send.at[0], h_recv.at[0], below
    )
    halo_up = remote(
        fr.at[1, :, :, pl.ds(0, R)], fr.at[BANDS + 1, :, :, pl.ds(0, R)], h_send.at[1], h_recv.at[1], above
    )

    def finish(b):
        landed(fr.at[band(2 * b) + 1], f_recv.at[b])

        @pl.when((b == 0) & has_below & jnp.logical_not(seam_below))
        def _():
            halo_down.start()

        @pl.when((b == 1) & has_above & jnp.logical_not(seam_above))
        def _():
            halo_up.start()

        @pl.when((b == 2) & seam_below)
        def _():
            pl.when(has_right)(functools.partial(pl.semaphore_wait, go_all, 1))
            halo_down.start()

        @pl.when((b == 2) & seam_above)
        def _():
            pl.when(has_left)(functools.partial(pl.semaphore_wait, go_all, 1))
            halo_up.start()

        @pl.when(b >= 3)
        def _():
            low_pass(b - 2)

    def collect(c):
        for s in range(HALF):
            fin[c // 2, :, HALF * (c % 2) + s] = p_buf[c, z, s]

        @pl.when(c % 2 == 1)
        def _():
            b = c // 2
            slot = fr.at[band(c) + 1, me]
            for step in range(1, OWNERS):
                owner = (me + step) % OWNERS
                remote(fin.at[b, pl.ds(KEEP * owner, KEEP)], slot, f_send, f_recv.at[b], peer(owner)).start()
            pltpu.make_async_copy(fin.at[b, pl.ds(KEEP * me, KEEP)], slot, f_recv.at[b]).start()

            for gate, across, way in ((gate_below, gate_to_below, 1), (gate_above, gate_to_above, -1)):
                pl.when(gate & (b == 0))(functools.partial(signal, go_line, across))

                @pl.when(gate & (b == 1))
                def _():
                    pl.semaphore_wait(go_line, 1)
                    for hops in range(1, LINE):
                        signal(go_all, {"stack": stack - 2 * hops * way})

            @pl.when((b >= 1) & (b <= WHOLE // 2))
            def _():
                finish(b - 1)

    items = (LINE - 1) * (CHUNKS + 1)
    first = (LINE - 1) * UNITS

    def place(item):
        late = (item >= first).astype(jnp.int32)
        unit = (item * 9363) >> 16
        after = item - first
        head = (unit > 0).astype(jnp.int32)
        return (
            late * (WHOLE + (after & 7)) + (1 - late) * (unit - head),
            late * (after >> 3) + (1 - late) * (item - (LINE - 1) * unit),
            late * (UNITS + (after & 7)) + (1 - late) * unit,
            late * (after & 7) + (1 - late) * unit,
        )

    def flow(t, p, way, ends):
        item = t - LAG * p

        @pl.when((item >= 0) & (item < items))
        def _():
            c, hop, unit, turn = place(item)
            left_over = LINE - 1 - hop - p
            d = way * hop + (1 - way) * (LINE - 1 - hop)
            plain = c >= WHOLE

            if ends == 0:

                @pl.when(hop == 0)
                def _():
                    pl.when(unit != 1)(functools.partial(compute, c))

                    @pl.when(next_to_end)
                    def _():
                        pl.when(unit == 0)(functools.partial(compute_part, 0))
                        pl.when(unit == 1)(functools.partial(compute_part, 1))
                        pl.when((unit > 1) & (c < WHOLE))(functools.partial(compute_end, c))

            def travel(rows):
                @pl.when((p > 1) | ((p == 1) & plain))
                def _():
                    landed(s_buf.at[way, c, d, rows], s_recv.at[way, turn, hop])
                    p_buf[c, d, rows] = p_buf[c, d, rows] + s_buf[way, c, d, rows]

                @pl.when((left_over > 0) & ((p > 0) | plain))
                def _():
                    remote(
                        p_buf.at[c, d, rows], s_buf.at[way, c, d, rows], s_send.at[way], s_recv.at[way, turn, hop],
                        onward(way),
                    ).start()

            @pl.when(left_over >= 0)
            def _():
                @pl.when(unit < 2)
                def _():
                    travel(pl.ds(HALF // 2 * unit, HALF // 2))

                @pl.when(unit >= 2)
                def _():
                    travel(pl.ds(0, HALF))

                last = (left_over == 0) & (unit > 0)

                @pl.when(last & ((jnp.logical_not(plain) | at_end) if ends else plain))
                def _():
                    collect(c)

    def step(t, carry):
        flow(t, near, half, 0)
        flow(t, LINE - 1 - near, 1 - half, 1)
        return carry

    steps = max(items + LAG, first + CHUNKS - WHOLE + (LINE - 1) * LAG)
    lax.fori_loop(0, steps, step, 0)

    def rest(b, carry):
        finish(b)
        return carry

    lax.fori_loop(WHOLE // 2, BANDS - 1, rest, 0)

    @pl.when(has_above)
    def _():
        halo_down.wait_recv()
        halo_up.wait_send()

    @pl.when(has_below)
    def _():
        halo_up.wait_recv()
        halo_down.wait_send()

    low_pass(0)
    finish(BANDS - 1)

    def tail(q, carry):
        low_pass(q)
        return carry

    lax.fori_loop(BANDS - 2, BANDS, tail, 0)

    landed(x_buf.at[:, pl.ds(0, (OWNERS - 1) * DEPTH)], x_send)
    landed(fr.at[pl.ds(1, BANDS), pl.ds(0, OWNERS - 1)], f_send)
    pl.when(at_end)(functools.partial(landed, y_buf, y_send))
    for way, p in ((0, z), (1, mirror)):
        for k in range(LINE - 1):
            chunks = pl.ds(0, CHUNKS) if k else pl.ds(WHOLE, CHUNKS - WHOLE)
            ahead = p_buf.at[chunks, pl.ds(0, LINE - 1 - k)]
            pl.when(p == k)(functools.partial(landed, ahead, s_send.at[way]))


def shards(interferograms, pairs):
    dma = pltpu.SemaphoreType.DMA
    block = (CHUNKS, LINE, HALF, SHARE, LANES)
    held = (BANDS, DEPTH * OWNERS, 8, LANES)
    return pl.pallas_call(
        kernel,
        out_shape=pltpu.VMEM((KEEP,) + interferograms.shape[1:], f32),
        in_specs=[pl.BlockSpec(memory_space=pltpu.HBM), pl.BlockSpec(memory_space=pltpu.VMEM)],
        out_specs=pl.BlockSpec(memory_space=pltpu.VMEM),
        scratch_shapes=[
            pltpu.VMEM(held, f32),
            pltpu.VMEM((WHOLE // 2,) + held[1:], f32),
            pltpu.VMEM(block, f32),
            pltpu.VMEM((2,) + block, f32),
            pltpu.VMEM((BANDS, SHARE, 8, LANES), f32),
            pltpu.VMEM((BANDS + 2, OWNERS, KEEP, 8, LANES), f32),
            pltpu.VMEM((PAD, 1024), bf16),
            pltpu.VMEM((2 * PAD, PAD), f32),
            pltpu.VMEM((ND, 2 * LANES), bf16),
            pltpu.VMEM((ND, LANES), bf16),
            pltpu.VMEM((ND, 2 * LANES), bf16),
            pltpu.VMEM((ND, LANES), bf16),
            dma, dma((CHUNKS,)),
            dma, dma((UNITS,)),
            dma((2,)), dma((2, UNITS, LINE - 1)),
            dma, dma((BANDS,)),
            dma((2,)), dma((2,)),
            pltpu.SemaphoreType.REGULAR, pltpu.SemaphoreType.REGULAR,
        ],
        compiler_params=pltpu.CompilerParams(
            collective_id=0, has_side_effects=True, vmem_limit_bytes=61 * 1024 * 1024
        ),
    )(interferograms, pairs.T)


def solution(mesh):
    return jax.shard_map(
        shards,
        mesh=mesh,
        in_specs=(P("stack", "rows", None), P()),
        out_specs=P("stack", "rows", None),
        check_vma=False,
    )
```

```python
import functools

import jax
import jax.numpy as jnp
import numpy as np
from jax import lax
from jax.experimental import pallas as pl
from jax.experimental.pallas import tpu as pltpu
from jax.sharding import PartitionSpec as P

ND = 192
R = 4
TIKHONOV = 0.1
TEMPORAL_SIGMA = 6.0
SPATIAL_SIGMA = 1.5

LINE = 8
OWNERS = 8
DEPTH = 16
LANES = 128
BANDS = 8
CHUNKS = 16
HALF = 4
UNITS = 9
SHARE = ND // LINE
KEEP = ND // (LINE * OWNERS)
PAD = 256
WHOLE = 8
LAG = 6
RELAY = 95
AHEAD = 6
DIRECT = 2
ROUNDS = 9
f32 = jnp.float32
bf16 = jnp.bfloat16


def spatial_taps():
    offsets = np.arange(-R, R + 1).astype(np.float32) / np.float32(SPATIAL_SIGMA)
    taps = np.exp(np.float32(-0.5) * offsets * offsets)
    return [float(tap) for tap in (taps / np.sum(taps)).astype(np.float32)]


def dot(a, b):
    return jnp.dot(a, b, preferred_element_type=f32)


def two(a):
    high = a.astype(bf16)
    return high, (a - high.astype(f32)).astype(bf16)


def dot3(a, b):
    ah, al = two(a)
    bh, bl = two(b)
    return dot(ah, bh) + (dot(ah, bl) + dot(al, bh))


def dot6(a, b):
    return jnp.dot(a, b, precision=lax.Precision.HIGHEST, preferred_element_type=f32)


def inverse(normal, eye, ex):
    top = jnp.max(jnp.sum(jnp.abs(normal), axis=1, keepdims=True), axis=0, keepdims=True)
    scale = 2.0 / (top + TIKHONOV)
    ex[0:PAD] = eye - scale * normal
    ex[PAD : 2 * PAD] = scale * eye

    def turn(_, rho):
        both = ex[...]
        err = both[0:PAD]
        product = dot3(both, err)
        gain = 2.0 / (2.0 - rho * rho)
        ex[0:PAD] = gain * product[0:PAD] + (1.0 - gain) * eye
        ex[PAD : 2 * PAD] = gain * (both[PAD : 2 * PAD] + product[PAD : 2 * PAD])
        return 0.5 * rho * rho * gain

    lax.fori_loop(0, ROUNDS, turn, (top - TIKHONOV) / (top + TIKHONOV))

    def polish(_, carry):
        now = ex[PAD : 2 * PAD]
        left = eye - dot6(normal, now)
        ex[PAD : 2 * PAD] = now + dot3(now, left)
        return carry

    lax.fori_loop(0, 3, polish, 0)
    return ex[PAD : 2 * PAD]


def network(pairs):
    dates = lax.broadcasted_iota(jnp.int32, (PAD, pairs.shape[1]), 0)
    design = (dates == pairs[1:2, :]).astype(f32) - (dates == pairs[0:1, :]).astype(f32)
    design = design.astype(bf16)
    return design, lax.dot_general(design, design, (((1,), (1,)), ((), ())), preferred_element_type=f32)


def tables(z, end, next_to_end, pairs, design_ref, ex, q_high, q_low, e_high, e_low):
    design = design_ref[...]
    row = lax.broadcasted_iota(jnp.int32, (PAD, PAD), 0)
    col = lax.broadcasted_iota(jnp.int32, (PAD, PAD), 1)
    eye = (row == col).astype(f32)
    normal = ex[0:PAD] + TIKHONOV * eye
    solved = inverse(normal, eye, ex)
    at_z = (row * 2731) >> 16
    rest = row - SHARE * at_z
    at_x = (rest * 43) >> 8
    date = 48 * at_x + 6 * at_z + (rest - 6 * at_x)
    offset = (date - col).astype(f32) / TEMPORAL_SIGMA
    weight = jnp.where(col < ND, jnp.exp(-0.5 * offset * offset), 0.0)
    smooth = weight / jnp.sum(weight, axis=1, keepdims=True)
    change = dot6((date == col).astype(f32) - smooth, solved)
    first = change.astype(bf16)
    rest = change - first.astype(f32)
    second = rest.astype(bf16)
    third = (rest - second.astype(f32)).astype(bf16)
    k = lax.broadcasted_iota(jnp.int32, (pairs.shape[1], LANES), 0)
    j = lax.broadcasted_iota(jnp.int32, (pairs.shape[1], LANES), 1)

    def held(at):
        pick = (k == 256 * (j >> 5) + 32 * at + (j & 31)).astype(f32).astype(bf16)
        mine = dot(design, pick).astype(bf16)
        return dot(first, mine) + (dot(second, mine) + dot(third, mine))

    def keep(q, high_ref, low_ref):
        high, low = two(q[0:ND])
        high_ref[...] = jnp.concatenate([high, high], axis=1)
        low_ref[...] = low

    keep(held(z), q_high, q_low)

    @pl.when(next_to_end)
    def _():
        keep(jnp.where(at_z[:, 0:LANES] == end, 0.0, held(end)), e_high, e_low)


def kernel(
    ifg, pairs, out, x_buf, y_buf, p_buf, s_buf, fin, fr, design_ref, ex, q_high, q_low, e_high, e_low,
    x_send, x_recv, y_send, y_recv, s_send, s_recv, f_send, f_recv, h_send, h_recv, go_line, go_all, relay, relay_send, relay_recv,
):
    stack = lax.axis_index("stack")
    slab = lax.axis_index("rows")
    slabs = lax.axis_size("rows")
    x = stack // (2 * LINE)
    z = (stack // 2) % LINE
    core = stack % 2
    me = 2 * x + core
    mirror = LINE - 1 - z
    half = z // (LINE // 2)
    near = z * (1 - half) + mirror * half
    end = (LINE - 1) * half
    at_end, next_to_end = near == 0, near == 1

    def peer(owner):
        return {"stack": 2 * LINE * (owner // 2) + 2 * z + owner % 2}

    def remote(src, dst, send, recv, device):
        return pltpu.make_async_remote_copy(
            src_ref=src, dst_ref=dst, send_sem=send, recv_sem=recv,
            device_id=device, device_id_type=pl.DeviceIdType.MESH,
        )

    def landed(ref, sem):
        pltpu.make_async_copy(ref, ref, sem).wait()

    def onward(way):
        return {"stack": stack + 2 - 4 * way}

    below = {"rows": slab + 1}
    above = {"rows": slab - 1}
    has_left, has_right = z > 0, z < LINE - 1
    has_above, has_below = slab > 0, slab < slabs - 1
    seam_below, seam_above = slab == slabs // 2 - 1, slab == slabs // 2
    gate_below, gate_above = seam_below & (z == LINE - 1), seam_above & (z == 0)
    gate_to_below = {"stack": stack - 2 * (LINE - 1), "rows": slab + 1}
    gate_to_above = {"stack": stack + 2 * (LINE - 1), "rows": slab - 1}

    barrier = pltpu.get_barrier_semaphore()

    def signal(sem, device):
        pl.semaphore_signal(sem, inc=1, device_id=device, device_id_type=pl.DeviceIdType.MESH)

    def beside(owner, way):
        return {"stack": 2 * LINE * (owner // 2) + 2 * (z + 1 - 2 * way) + owner % 2}

    for step in range(1, OWNERS):
        signal(barrier, peer((me + step) % OWNERS))
    count = OWNERS - 1
    ends_pair = at_end | next_to_end
    pair_way = half * at_end.astype(jnp.int32) + (1 - half) * next_to_end.astype(jnp.int32)

    @pl.when(ends_pair)
    def _():
        for step in range(1, OWNERS):
            signal(barrier, beside((me + step) % OWNERS, pair_way))

    count = count + (OWNERS - 1) * ends_pair.astype(jnp.int32)
    for there, device in (
        (has_left, onward(1)),
        (has_right, onward(0)),
        (has_above & jnp.logical_not(seam_above), above),
        (has_below & jnp.logical_not(seam_below), below),
        (gate_above, gate_to_above),
        (gate_below, gate_to_below),
    ):
        pl.when(there)(functools.partial(signal, barrier, device))
        count = count + there.astype(jnp.int32)
    design_ref[...], ex[0:PAD] = network(pairs)
    pl.semaphore_wait(barrier, count)

    def band(c):
        return (c // 2 + BANDS - 1) % BANDS

    def half_rows(c):
        return pl.ds(HALF * (c % 2), HALF)

    def x_piece(c, owner):
        rows = pl.ds(8 * band(c) + HALF * (c % 2), HALF)
        return ifg.at[:, rows, pl.ds(pl.multiple_of(LANES * owner, LANES), LANES)]

    def x_slot(c):
        return x_buf.at[c // 2, pl.ds(DEPTH * me, DEPTH), half_rows(c)]

    def spread(c, carry):
        for step in range(1, OWNERS):
            owner = (me + step) % OWNERS
            remote(x_piece(c, owner), x_slot(c), x_send, x_recv.at[c], peer(owner)).start()
        pltpu.make_async_copy(x_piece(c, me), x_slot(c), x_recv.at[c]).start()
        return carry

    def x_landed(c):
        landed(x_buf.at[c // 2, :, half_rows(c)], x_recv.at[c])

    def whole(c, device):
        return remote(
            x_buf.at[c // 2, :, half_rows(c)], y_buf.at[c // 2, :, half_rows(c)], y_send, y_recv.at[c + 1], device
        )

    def spread_direct(unit, band_row, height):
        for step in range(OWNERS):
            owner = (me + step) % OWNERS
            piece = ifg.at[
                :, pl.ds(8 * band(0) + band_row, height), pl.ds(pl.multiple_of(LANES * owner, LANES), LANES)
            ]
            slot = y_buf.at[0, pl.ds(DEPTH * me, DEPTH), pl.ds(band_row, height)]
            remote(piece, slot, y_send, y_recv.at[unit], beside(owner, half)).start()

    @pl.when(at_end)
    def _():
        spread_direct(0, 0, HALF // 2)
        spread_direct(1, HALF // 2, HALF // 2)
        spread_direct(2, HALF, HALF)

    lax.fori_loop(0, AHEAD, spread, 0)

    def spread_next(c):
        @pl.when(2 * c + AHEAD < CHUNKS)
        def _():
            spread(2 * c + AHEAD, 0)
            spread(2 * c + AHEAD + 1, 0)

    @pl.when(at_end)
    def _():
        def pass_on(c, carry):
            x_landed(c)

            @pl.when(c >= DIRECT)
            def _():
                whole(c, onward(half)).start()

            spread_next(c)
            return carry

        lax.fori_loop(0, WHOLE, pass_on, 0)

    tables(z, end, next_to_end, pairs, design_ref, ex, q_high, q_low, e_high, e_low)

    @pl.when(jnp.logical_not(has_above))
    def _():
        fr[0] = jnp.zeros(fr.shape[1:], f32)

    @pl.when(jnp.logical_not(has_below))
    def _():
        fr[BANDS + 1] = jnp.zeros(fr.shape[1:], f32)

    taps = spatial_taps()

    def multiply(c, source, high_ref, low_ref, more, rows=range(0, HALF, 2)):
        for s in rows:
            at = HALF * (c % 2) + s
            block = jnp.concatenate([source[c // 2, :, at], source[c // 2, :, at + 1]], axis=1)
            high, low = two(block)
            product = dot(high_ref[...], jnp.concatenate([high, low], axis=0)) + dot(low_ref[...], high)
            for t in range(2):
                part = product[:, LANES * t : LANES * (t + 1)].reshape(LINE, SHARE, LANES)
                p_buf[c, :, s + t] = part + p_buf[c, :, s + t] if more else part

    def compute(c):
        @pl.when(jnp.logical_not(at_end & (c < WHOLE)))
        def _():
            x_landed(c)
            spread_next(c)

        multiply(c, x_buf, q_high, q_low, False)

    def compute_end(c):
        landed(y_buf.at[c // 2, :, half_rows(c)], y_recv.at[c + 1])
        multiply(c, y_buf, e_high, e_low, True)

    def compute_part(unit):
        landed(y_buf.at[0, :, pl.ds(HALF // 2 * unit, HALF // 2)], y_recv.at[unit])
        multiply(0, y_buf, e_high, e_low, True, (HALF // 2 * unit,))

    def low_pass(q):
        lane = lax.broadcasted_iota(jnp.int32, (8, LANES * OWNERS), 1)
        for i in range(KEEP):
            window = jnp.concatenate(
                [fr[q, :, i, 8 - R : 8], fr[q + 1, :, i], fr[q + 2, :, i, 0:R]], axis=1
            )
            rowpass = taps[R] * window[:, R : R + 8]
            for s in range(1, R + 1):
                rowpass = rowpass + taps[R + s] * (
                    window[:, R - s : R - s + 8] + window[:, R + s : R + s + 8]
                )
            line = jnp.concatenate([rowpass[o] for o in range(OWNERS)], axis=1)
            total = taps[R] * line
            width = LANES * OWNERS
            for s in range(1, R + 1):
                before = jnp.where(lane >= s, pltpu.roll(line, s, 1), 0.0)
                after = jnp.where(lane < width - s, pltpu.roll(line, width - s, 1), 0.0)
                total = total + taps[R + s] * (before + after)
            out[i, pl.ds(pl.multiple_of(8 * q, 8), 8)] = total

    halo_down = remote(
        fr.at[BANDS, :, :, pl.ds(8 - R, R)], fr.at[0, :, :, pl.ds(8 - R, R)], h_send.at[0], h_recv.at[0], below
    )
    halo_up = remote(
        fr.at[1, :, :, pl.ds(0, R)], fr.at[BANDS + 1, :, :, pl.ds(0, R)], h_send.at[1], h_recv.at[1], above
    )

    halfway = stack + 4 * 2 * (1 - 2 * half)
    lower, upper = pl.ds(8 - R, R), pl.ds(0, R)
    seam_down = remote(
        fr.at[BANDS, :, :, lower], relay.at[:, :, lower], h_send.at[0], relay_recv, {"stack": halfway}
    )
    seam_down_on = remote(
        relay.at[:, :, lower], fr.at[0, :, :, lower], relay_send, h_recv.at[0], {"stack": halfway, "rows": slab + 1}
    )
    seam_up = remote(fr.at[1, :, :, upper], relay.at[:, :, upper], h_send.at[1], relay_recv, {"stack": halfway})
    seam_up_on = remote(
        relay.at[:, :, upper], fr.at[BANDS + 1, :, :, upper], relay_send, h_recv.at[1],
        {"stack": halfway, "rows": slab - 1},
    )

    def finish(b):
        landed(fr.at[band(2 * b) + 1], f_recv.at[b])

        @pl.when((b == 0) & has_below & jnp.logical_not(seam_below))
        def _():
            halo_down.start()

        @pl.when((b == 1) & has_above & jnp.logical_not(seam_above))
        def _():
            halo_up.start()

        @pl.when((b == 1) & seam_below)
        def _():
            pl.when(has_right)(functools.partial(pl.semaphore_wait, go_all, 1))
            seam_down.start()

        @pl.when((b == 1) & seam_above)
        def _():
            pl.when(has_left)(functools.partial(pl.semaphore_wait, go_all, 1))
            seam_up.start()

        @pl.when(b >= 3)
        def _():
            low_pass(b - 2)

    def collect(c):
        for s in range(HALF):
            fin[c // 2, :, HALF * (c % 2) + s] = p_buf[c, z, s]

        for gate, way in ((gate_below, 1), (gate_above, -1)):

            @pl.when(gate & (c == 2))
            def _():
                pl.semaphore_wait(go_line, 1)
                for hops in range(1, LINE):
                    signal(go_all, {"stack": stack - 2 * hops * way})

        @pl.when(c % 2 == 1)
        def _():
            b = c // 2
            slot = fr.at[band(c) + 1, me]
            for step in range(1, OWNERS):
                owner = (me + step) % OWNERS
                remote(fin.at[b, pl.ds(KEEP * owner, KEEP)], slot, f_send, f_recv.at[b], peer(owner)).start()
            pltpu.make_async_copy(fin.at[b, pl.ds(KEEP * me, KEEP)], slot, f_recv.at[b]).start()

            for gate, across in ((gate_below, gate_to_below), (gate_above, gate_to_above)):
                pl.when(gate & (b == 0))(functools.partial(signal, go_line, across))

            @pl.when((b >= 1) & (b <= WHOLE // 2))
            def _():
                finish(b - 1)

    items = (LINE - 1) * (CHUNKS + 1)
    first = (LINE - 1) * UNITS

    def place(item):
        late = (item >= first).astype(jnp.int32)
        unit = (item * 9363) >> 16
        after = item - first
        head = (unit > 0).astype(jnp.int32)
        return (
            late * (WHOLE + (after & 7)) + (1 - late) * (unit - head),
            late * (after >> 3) + (1 - late) * (item - (LINE - 1) * unit),
            late * (UNITS + (after & 7)) + (1 - late) * unit,
            late * (after & 7) + (1 - late) * unit,
        )

    def flow(t, p, way, ends):
        item = t - LAG * p

        @pl.when((item >= 0) & (item < items))
        def _():
            c, hop, unit, turn = place(item)
            left_over = LINE - 1 - hop - p
            d = way * hop + (1 - way) * (LINE - 1 - hop)
            plain = c >= WHOLE

            if ends == 0:

                @pl.when(hop == 0)
                def _():
                    pl.when(unit != 1)(functools.partial(compute, c))

                    @pl.when(next_to_end)
                    def _():
                        pl.when(unit == 0)(functools.partial(compute_part, 0))
                        pl.when(unit == 1)(functools.partial(compute_part, 1))
                        pl.when((unit > 1) & (c < WHOLE))(functools.partial(compute_end, c))

            def travel(rows):
                @pl.when((p > 1) | ((p == 1) & plain))
                def _():
                    landed(s_buf.at[way, c, d, rows], s_recv.at[way, turn, hop])
                    p_buf[c, d, rows] = p_buf[c, d, rows] + s_buf[way, c, d, rows]

                @pl.when((left_over > 0) & ((p > 0) | plain))
                def _():
                    remote(
                        p_buf.at[c, d, rows], s_buf.at[way, c, d, rows], s_send.at[way], s_recv.at[way, turn, hop],
                        onward(way),
                    ).start()

            @pl.when(left_over >= 0)
            def _():
                @pl.when(unit < 2)
                def _():
                    travel(pl.ds(HALF // 2 * unit, HALF // 2))

                @pl.when(unit >= 2)
                def _():
                    travel(pl.ds(0, HALF))

                last = (left_over == 0) & (unit > 0)

                @pl.when(last & ((jnp.logical_not(plain) | at_end) if ends else plain))
                def _():
                    collect(c)

    def step(t, carry):
        flow(t, near, half, 0)
        flow(t, LINE - 1 - near, 1 - half, 1)

        for there, first_leg, second_leg in ((seam_below, seam_down, seam_down_on), (seam_above, seam_up, seam_up_on)):

            @pl.when(there & (t == RELAY))
            def _():
                first_leg.wait_recv()
                second_leg.start()

        return carry

    steps = max(items + LAG, first + CHUNKS - WHOLE + (LINE - 1) * LAG)
    lax.fori_loop(0, steps, step, 0)

    def rest(b, carry):
        finish(b)
        return carry

    lax.fori_loop(WHOLE // 2, BANDS - 1, rest, 0)

    @pl.when(has_above)
    def _():
        halo_down.wait_recv()
        halo_up.wait_send()

    @pl.when(has_below)
    def _():
        halo_up.wait_recv()
        halo_down.wait_send()

    low_pass(0)
    finish(BANDS - 1)

    def tail(q, carry):
        low_pass(q)
        return carry

    lax.fori_loop(BANDS - 2, BANDS, tail, 0)

    pl.when(seam_below)(seam_down_on.wait_send)
    pl.when(seam_above)(seam_up_on.wait_send)

    landed(x_buf.at[:, pl.ds(0, (OWNERS - 1) * DEPTH)], x_send)
    landed(fr.at[pl.ds(1, BANDS), pl.ds(0, OWNERS - 1)], f_send)
    pl.when(at_end)(functools.partial(landed, y_buf, y_send))
    for way, p in ((0, z), (1, mirror)):
        for k in range(LINE - 1):
            chunks = pl.ds(0, CHUNKS) if k else pl.ds(WHOLE, CHUNKS - WHOLE)
            ahead = p_buf.at[chunks, pl.ds(0, LINE - 1 - k)]
            pl.when(p == k)(functools.partial(landed, ahead, s_send.at[way]))


def shards(interferograms, pairs):
    dma = pltpu.SemaphoreType.DMA
    block = (CHUNKS, LINE, HALF, SHARE, LANES)
    held = (BANDS, DEPTH * OWNERS, 8, LANES)
    return pl.pallas_call(
        kernel,
        out_shape=pltpu.VMEM((KEEP,) + interferograms.shape[1:], f32),
        in_specs=[pl.BlockSpec(memory_space=pltpu.HBM), pl.BlockSpec(memory_space=pltpu.VMEM)],
        out_specs=pl.BlockSpec(memory_space=pltpu.VMEM),
        scratch_shapes=[
            pltpu.VMEM(held, f32),
            pltpu.VMEM((WHOLE // 2,) + held[1:], f32),
            pltpu.VMEM(block, f32),
            pltpu.VMEM((2,) + block, f32),
            pltpu.VMEM((BANDS, SHARE, 8, LANES), f32),
            pltpu.VMEM((BANDS + 2, OWNERS, KEEP, 8, LANES), f32),
            pltpu.VMEM((PAD, 1024), bf16),
            pltpu.VMEM((2 * PAD, PAD), f32),
            pltpu.VMEM((ND, 2 * LANES), bf16),
            pltpu.VMEM((ND, LANES), bf16),
            pltpu.VMEM((ND, 2 * LANES), bf16),
            pltpu.VMEM((ND, LANES), bf16),
            dma, dma((CHUNKS,)),
            dma, dma((UNITS,)),
            dma((2,)), dma((2, UNITS, LINE - 1)),
            dma, dma((BANDS,)),
            dma((2,)), dma((2,)),
            pltpu.SemaphoreType.REGULAR, pltpu.SemaphoreType.REGULAR,
            pltpu.VMEM((OWNERS, KEEP, 8, LANES), f32), dma, dma,
        ],
        compiler_params=pltpu.CompilerParams(
            collective_id=0, has_side_effects=True, vmem_limit_bytes=61 * 1024 * 1024
        ),
    )(interferograms, pairs.T)


def solution(mesh):
    return jax.shard_map(
        shards,
        mesh=mesh,
        in_specs=(P("stack", "rows", None), P()),
        out_specs=P("stack", "rows", None),
        check_vma=False,
    )
```

```python
import functools

import jax
import jax.numpy as jnp
import numpy as np
from jax import lax
from jax.experimental import pallas as pl
from jax.experimental.pallas import tpu as pltpu
from jax.sharding import PartitionSpec as P

ND = 192
R = 4
TIKHONOV = 0.1
TEMPORAL_SIGMA = 6.0
SPATIAL_SIGMA = 1.5

LINE = 8
OWNERS = 8
DEPTH = 16
LANES = 128
BANDS = 8
CHUNKS = 16
HALF = 4
UNITS = 9
SHARE = ND // LINE
KEEP = ND // (LINE * OWNERS)
PAD = 256
WHOLE = 8
LAG = 7
RELAY = 95
AHEAD = 6
DIRECT = 2
ROUNDS = 9
f32 = jnp.float32
bf16 = jnp.bfloat16


def spatial_taps():
    offsets = np.arange(-R, R + 1).astype(np.float32) / np.float32(SPATIAL_SIGMA)
    taps = np.exp(np.float32(-0.5) * offsets * offsets)
    return [float(tap) for tap in (taps / np.sum(taps)).astype(np.float32)]


def dot(a, b):
    return jnp.dot(a, b, preferred_element_type=f32)


def two(a):
    high = a.astype(bf16)
    return high, (a - high.astype(f32)).astype(bf16)


def dot3(a, b):
    ah, al = two(a)
    bh, bl = two(b)
    return dot(ah, bh) + (dot(ah, bl) + dot(al, bh))


def dot6(a, b):
    return jnp.dot(a, b, precision=lax.Precision.HIGHEST, preferred_element_type=f32)


def inverse(normal, eye, ex):
    top = jnp.max(jnp.sum(jnp.abs(normal), axis=1, keepdims=True), axis=0, keepdims=True)
    scale = 2.0 / (top + TIKHONOV)
    ex[0:PAD] = eye - scale * normal
    ex[PAD : 2 * PAD] = scale * eye

    def turn(_, rho):
        both = ex[...]
        err = both[0:PAD]
        product = dot3(both, err)
        gain = 2.0 / (2.0 - rho * rho)
        ex[0:PAD] = gain * product[0:PAD] + (1.0 - gain) * eye
        ex[PAD : 2 * PAD] = gain * (both[PAD : 2 * PAD] + product[PAD : 2 * PAD])
        return 0.5 * rho * rho * gain

    lax.fori_loop(0, ROUNDS, turn, (top - TIKHONOV) / (top + TIKHONOV))

    def polish(_, carry):
        now = ex[PAD : 2 * PAD]
        left = eye - dot6(normal, now)
        ex[PAD : 2 * PAD] = now + dot3(now, left)
        return carry

    lax.fori_loop(0, 3, polish, 0)
    return ex[PAD : 2 * PAD]


def network(pairs):
    dates = lax.broadcasted_iota(jnp.int32, (PAD, pairs.shape[1]), 0)
    design = (dates == pairs[1:2, :]).astype(f32) - (dates == pairs[0:1, :]).astype(f32)
    design = design.astype(bf16)
    return design, lax.dot_general(design, design, (((1,), (1,)), ((), ())), preferred_element_type=f32)


def tables(z, end, next_to_end, pairs, design_ref, ex, q_high, q_low, e_high, e_low):
    design = design_ref[...]
    row = lax.broadcasted_iota(jnp.int32, (PAD, PAD), 0)
    col = lax.broadcasted_iota(jnp.int32, (PAD, PAD), 1)
    eye = (row == col).astype(f32)
    normal = ex[0:PAD] + TIKHONOV * eye
    solved = inverse(normal, eye, ex)
    at_z = (row * 2731) >> 16
    rest = row - SHARE * at_z
    at_x = (rest * 43) >> 8
    date = 48 * at_x + 6 * at_z + (rest - 6 * at_x)
    offset = (date - col).astype(f32) / TEMPORAL_SIGMA
    weight = jnp.where(col < ND, jnp.exp(-0.5 * offset * offset), 0.0)
    smooth = weight / jnp.sum(weight, axis=1, keepdims=True)
    change = dot6((date == col).astype(f32) - smooth, solved)
    first = change.astype(bf16)
    rest = change - first.astype(f32)
    second = rest.astype(bf16)
    third = (rest - second.astype(f32)).astype(bf16)
    k = lax.broadcasted_iota(jnp.int32, (pairs.shape[1], LANES), 0)
    j = lax.broadcasted_iota(jnp.int32, (pairs.shape[1], LANES), 1)

    def held(at):
        pick = (k == 256 * (j >> 5) + 32 * at + (j & 31)).astype(f32).astype(bf16)
        mine = dot(design, pick).astype(bf16)
        return dot(first, mine) + (dot(second, mine) + dot(third, mine))

    def keep(q, high_ref, low_ref):
        high, low = two(q[0:ND])
        high_ref[...] = jnp.concatenate([high, high], axis=1)
        low_ref[...] = low

    keep(held(z), q_high, q_low)

    @pl.when(next_to_end)
    def _():
        keep(jnp.where(at_z[:, 0:LANES] == end, 0.0, held(end)), e_high, e_low)


def kernel(
    ifg, pairs, out, x_buf, y_buf, p_buf, s_buf, fin, fr, design_ref, ex, q_high, q_low, e_high, e_low,
    x_send, x_recv, y_send, y_recv, s_send, s_recv, f_send, f_recv, h_send, h_recv, go_line, go_all, relay, relay_send, relay_recv,
):
    stack = lax.axis_index("stack")
    slab = lax.axis_index("rows")
    slabs = lax.axis_size("rows")
    x = stack // (2 * LINE)
    z = (stack // 2) % LINE
    core = stack % 2
    me = 2 * x + core
    mirror = LINE - 1 - z
    half = z // (LINE // 2)
    near = z * (1 - half) + mirror * half
    end = (LINE - 1) * half
    at_end, next_to_end = near == 0, near == 1

    def peer(owner):
        return {"stack": 2 * LINE * (owner // 2) + 2 * z + owner % 2}

    def remote(src, dst, send, recv, device):
        return pltpu.make_async_remote_copy(
            src_ref=src, dst_ref=dst, send_sem=send, recv_sem=recv,
            device_id=device, device_id_type=pl.DeviceIdType.MESH,
        )

    def landed(ref, sem):
        pltpu.make_async_copy(ref, ref, sem).wait()

    def onward(way):
        return {"stack": stack + 2 - 4 * way}

    below = {"rows": slab + 1}
    above = {"rows": slab - 1}
    has_left, has_right = z > 0, z < LINE - 1
    has_above, has_below = slab > 0, slab < slabs - 1
    seam_below, seam_above = slab == slabs // 2 - 1, slab == slabs // 2
    gate_below, gate_above = seam_below & (z == LINE - 1), seam_above & (z == 0)
    gate_to_below = {"stack": stack - 2 * (LINE - 1), "rows": slab + 1}
    gate_to_above = {"stack": stack + 2 * (LINE - 1), "rows": slab - 1}

    barrier = pltpu.get_barrier_semaphore()

    def signal(sem, device):
        pl.semaphore_signal(sem, inc=1, device_id=device, device_id_type=pl.DeviceIdType.MESH)

    def beside(owner, way):
        return {"stack": 2 * LINE * (owner // 2) + 2 * (z + 1 - 2 * way) + owner % 2}

    for step in range(1, OWNERS):
        signal(barrier, peer((me + step) % OWNERS))
    count = OWNERS - 1
    ends_pair = at_end | next_to_end
    pair_way = half * at_end.astype(jnp.int32) + (1 - half) * next_to_end.astype(jnp.int32)

    @pl.when(ends_pair)
    def _():
        for step in range(1, OWNERS):
            signal(barrier, beside((me + step) % OWNERS, pair_way))

    count = count + (OWNERS - 1) * ends_pair.astype(jnp.int32)
    for there, device in (
        (has_left, onward(1)),
        (has_right, onward(0)),
        (has_above & jnp.logical_not(seam_above), above),
        (has_below & jnp.logical_not(seam_below), below),
        (gate_above, gate_to_above),
        (gate_below, gate_to_below),
    ):
        pl.when(there)(functools.partial(signal, barrier, device))
        count = count + there.astype(jnp.int32)
    design_ref[...], ex[0:PAD] = network(pairs)
    pl.semaphore_wait(barrier, count)

    def band(c):
        return (c // 2 + BANDS - 1) % BANDS

    def half_rows(c):
        return pl.ds(HALF * (c % 2), HALF)

    def x_piece(c, owner):
        rows = pl.ds(8 * band(c) + HALF * (c % 2), HALF)
        return ifg.at[:, rows, pl.ds(pl.multiple_of(LANES * owner, LANES), LANES)]

    def x_slot(c):
        return x_buf.at[c // 2, pl.ds(DEPTH * me, DEPTH), half_rows(c)]

    def spread(c, carry):
        for step in range(1, OWNERS):
            owner = (me + step) % OWNERS
            remote(x_piece(c, owner), x_slot(c), x_send, x_recv.at[c], peer(owner)).start()
        pltpu.make_async_copy(x_piece(c, me), x_slot(c), x_recv.at[c]).start()
        return carry

    def x_landed(c):
        landed(x_buf.at[c // 2, :, half_rows(c)], x_recv.at[c])

    def whole(c, device):
        return remote(
            x_buf.at[c // 2, :, half_rows(c)], y_buf.at[c // 2, :, half_rows(c)], y_send, y_recv.at[c + 1], device
        )

    def spread_direct(unit, band_row, height):
        for step in range(OWNERS):
            owner = (me + step) % OWNERS
            piece = ifg.at[
                :, pl.ds(8 * band(0) + band_row, height), pl.ds(pl.multiple_of(LANES * owner, LANES), LANES)
            ]
            slot = y_buf.at[0, pl.ds(DEPTH * me, DEPTH), pl.ds(band_row, height)]
            remote(piece, slot, y_send, y_recv.at[unit], beside(owner, half)).start()

    @pl.when(at_end)
    def _():
        spread_direct(0, 0, HALF // 2)
        spread_direct(1, HALF // 2, HALF // 2)
        spread_direct(2, HALF, HALF)

    lax.fori_loop(0, AHEAD, spread, 0)

    def spread_next(c):
        @pl.when(2 * c + AHEAD < CHUNKS)
        def _():
            spread(2 * c + AHEAD, 0)
            spread(2 * c + AHEAD + 1, 0)

    @pl.when(at_end)
    def _():
        def pass_on(c, carry):
            x_landed(c)

            @pl.when(c >= DIRECT)
            def _():
                whole(c, onward(half)).start()

            spread_next(c)
            return carry

        lax.fori_loop(0, WHOLE, pass_on, 0)

    tables(z, end, next_to_end, pairs, design_ref, ex, q_high, q_low, e_high, e_low)

    @pl.when(jnp.logical_not(has_above))
    def _():
        fr[0] = jnp.zeros(fr.shape[1:], f32)

    @pl.when(jnp.logical_not(has_below))
    def _():
        fr[BANDS + 1] = jnp.zeros(fr.shape[1:], f32)

    taps = spatial_taps()

    def multiply(c, source, high_ref, low_ref, more, rows=range(0, HALF, 2)):
        for s in rows:
            at = HALF * (c % 2) + s
            block = jnp.concatenate([source[c // 2, :, at], source[c // 2, :, at + 1]], axis=1)
            high, low = two(block)
            product = dot(high_ref[...], jnp.concatenate([high, low], axis=0)) + dot(low_ref[...], high)
            for t in range(2):
                part = product[:, LANES * t : LANES * (t + 1)].reshape(LINE, SHARE, LANES)
                p_buf[c, :, s + t] = part + p_buf[c, :, s + t] if more else part

    def compute(c):
        @pl.when(jnp.logical_not(at_end & (c < WHOLE)))
        def _():
            x_landed(c)
            spread_next(c)

        multiply(c, x_buf, q_high, q_low, False)

    def compute_end(c):
        landed(y_buf.at[c // 2, :, half_rows(c)], y_recv.at[c + 1])
        multiply(c, y_buf, e_high, e_low, True)

    def compute_part(unit):
        landed(y_buf.at[0, :, pl.ds(HALF // 2 * unit, HALF // 2)], y_recv.at[unit])
        multiply(0, y_buf, e_high, e_low, True, (HALF // 2 * unit,))

    def low_pass(q):
        lane = lax.broadcasted_iota(jnp.int32, (8, LANES * OWNERS), 1)
        for i in range(KEEP):
            window = jnp.concatenate(
                [fr[q, :, i, 8 - R : 8], fr[q + 1, :, i], fr[q + 2, :, i, 0:R]], axis=1
            )
            rowpass = taps[R] * window[:, R : R + 8]
            for s in range(1, R + 1):
                rowpass = rowpass + taps[R + s] * (
                    window[:, R - s : R - s + 8] + window[:, R + s : R + s + 8]
                )
            line = jnp.concatenate([rowpass[o] for o in range(OWNERS)], axis=1)
            total = taps[R] * line
            width = LANES * OWNERS
            for s in range(1, R + 1):
                before = jnp.where(lane >= s, pltpu.roll(line, s, 1), 0.0)
                after = jnp.where(lane < width - s, pltpu.roll(line, width - s, 1), 0.0)
                total = total + taps[R + s] * (before + after)
            out[i, pl.ds(pl.multiple_of(8 * q, 8), 8)] = total

    halo_down = remote(
        fr.at[BANDS, :, :, pl.ds(8 - R, R)], fr.at[0, :, :, pl.ds(8 - R, R)], h_send.at[0], h_recv.at[0], below
    )
    halo_up = remote(
        fr.at[1, :, :, pl.ds(0, R)], fr.at[BANDS + 1, :, :, pl.ds(0, R)], h_send.at[1], h_recv.at[1], above
    )

    halfway = stack + 4 * 2 * (1 - 2 * half)
    lower, upper = pl.ds(8 - R, R), pl.ds(0, R)
    seam_down = remote(
        fr.at[BANDS, :, :, lower], relay.at[:, :, lower], h_send.at[0], relay_recv, {"stack": halfway}
    )
    seam_down_on = remote(
        relay.at[:, :, lower], fr.at[0, :, :, lower], relay_send, h_recv.at[0], {"stack": halfway, "rows": slab + 1}
    )
    seam_up = remote(fr.at[1, :, :, upper], relay.at[:, :, upper], h_send.at[1], relay_recv, {"stack": halfway})
    seam_up_on = remote(
        relay.at[:, :, upper], fr.at[BANDS + 1, :, :, upper], relay_send, h_recv.at[1],
        {"stack": halfway, "rows": slab - 1},
    )

    def finish(b):
        landed(fr.at[band(2 * b) + 1], f_recv.at[b])

        @pl.when((b == 0) & has_below & jnp.logical_not(seam_below))
        def _():
            halo_down.start()

        @pl.when((b == 1) & has_above & jnp.logical_not(seam_above))
        def _():
            halo_up.start()

        @pl.when((b == 1) & seam_below)
        def _():
            pl.when(has_right)(functools.partial(pl.semaphore_wait, go_all, 1))
            seam_down.start()

        @pl.when((b == 1) & seam_above)
        def _():
            pl.when(has_left)(functools.partial(pl.semaphore_wait, go_all, 1))
            seam_up.start()

        @pl.when(b >= 3)
        def _():
            low_pass(b - 2)

    def collect(c):
        for s in range(HALF):
            fin[c // 2, :, HALF * (c % 2) + s] = p_buf[c, z, s]

        for gate, way in ((gate_below, 1), (gate_above, -1)):

            @pl.when(gate & (c == 2))
            def _():
                pl.semaphore_wait(go_line, 1)
                for hops in range(1, LINE):
                    signal(go_all, {"stack": stack - 2 * hops * way})

        @pl.when(c % 2 == 1)
        def _():
            b = c // 2
            slot = fr.at[band(c) + 1, me]
            for step in range(1, OWNERS):
                owner = (me + step) % OWNERS
                remote(fin.at[b, pl.ds(KEEP * owner, KEEP)], slot, f_send, f_recv.at[b], peer(owner)).start()
            pltpu.make_async_copy(fin.at[b, pl.ds(KEEP * me, KEEP)], slot, f_recv.at[b]).start()

            for gate, across in ((gate_below, gate_to_below), (gate_above, gate_to_above)):
                pl.when(gate & (b == 0))(functools.partial(signal, go_line, across))

            @pl.when((b >= 1) & (b <= WHOLE // 2))
            def _():
                finish(b - 1)

    items = (LINE - 1) * (CHUNKS + 1)
    first = (LINE - 1) * UNITS

    def place(item):
        late = (item >= first).astype(jnp.int32)
        unit = (item * 9363) >> 16
        after = item - first
        head = (unit > 0).astype(jnp.int32)
        return (
            late * (WHOLE + (after & 7)) + (1 - late) * (unit - head),
            late * (after >> 3) + (1 - late) * (item - (LINE - 1) * unit),
            late * (UNITS + (after & 7)) + (1 - late) * unit,
            late * (after & 7) + (1 - late) * unit,
        )

    def flow(t, p, way, ends):
        item = t - LAG * p

        @pl.when((item >= 0) & (item < items))
        def _():
            c, hop, unit, turn = place(item)
            left_over = LINE - 1 - hop - p
            d = way * hop + (1 - way) * (LINE - 1 - hop)
            row = hop + way * (LINE - 2 * hop)
            plain = c >= WHOLE

            if ends == 0:

                @pl.when(hop == 0)
                def _():
                    pl.when(unit != 1)(functools.partial(compute, c))

                    @pl.when(next_to_end)
                    def _():
                        pl.when(unit == 0)(functools.partial(compute_part, 0))
                        pl.when(unit == 1)(functools.partial(compute_part, 1))
                        pl.when((unit > 1) & (c < WHOLE))(functools.partial(compute_end, c))

            def travel(rows):
                @pl.when((p > 1) | ((p == 1) & plain))
                def _():
                    landed(s_buf.at[way, c, d, rows], s_recv.at[turn, row])
                    p_buf[c, d, rows] = p_buf[c, d, rows] + s_buf[way, c, d, rows]

                @pl.when((left_over > 0) & ((p > 0) | plain))
                def _():
                    remote(
                        p_buf.at[c, d, rows], s_buf.at[way, c, d, rows], s_send.at[way], s_recv.at[turn, row],
                        onward(way),
                    ).start()

            @pl.when(left_over >= 0)
            def _():
                @pl.when(unit < 2)
                def _():
                    travel(pl.ds(HALF // 2 * unit, HALF // 2))

                @pl.when(unit >= 2)
                def _():
                    travel(pl.ds(0, HALF))

                last = (left_over == 0) & (unit > 0)

                @pl.when(last & ((jnp.logical_not(plain) | at_end) if ends else plain))
                def _():
                    collect(c)

    def step(t, carry):
        flow(t, near, half, 0)
        flow(t, LINE - 1 - near, 1 - half, 1)

        for there, first_leg, second_leg in ((seam_below, seam_down, seam_down_on), (seam_above, seam_up, seam_up_on)):

            @pl.when(there & (t == RELAY))
            def _():
                first_leg.wait_recv()
                second_leg.start()

        return carry

    steps = max(items + LAG, first + CHUNKS - WHOLE + (LINE - 1) * LAG)
    lax.fori_loop(0, steps, step, 0)

    def rest(b, carry):
        finish(b)
        return carry

    lax.fori_loop(WHOLE // 2, BANDS - 1, rest, 0)

    @pl.when(has_above)
    def _():
        halo_down.wait_recv()
        halo_up.wait_send()

    @pl.when(has_below)
    def _():
        halo_up.wait_recv()
        halo_down.wait_send()

    low_pass(0)
    finish(BANDS - 1)

    def tail(q, carry):
        low_pass(q)
        return carry

    lax.fori_loop(BANDS - 2, BANDS, tail, 0)

    pl.when(seam_below)(seam_down_on.wait_send)
    pl.when(seam_above)(seam_up_on.wait_send)

    landed(x_buf.at[:, pl.ds(0, (OWNERS - 1) * DEPTH)], x_send)
    landed(fr.at[pl.ds(1, BANDS), pl.ds(0, OWNERS - 1)], f_send)
    pl.when(at_end)(functools.partial(landed, y_buf, y_send))
    for way, p in ((0, z), (1, mirror)):
        for k in range(LINE - 1):
            chunks = pl.ds(0, CHUNKS) if k else pl.ds(WHOLE, CHUNKS - WHOLE)
            ahead = p_buf.at[chunks, pl.ds(0, LINE - 1 - k)]
            pl.when(p == k)(functools.partial(landed, ahead, s_send.at[way]))


def shards(interferograms, pairs):
    dma = pltpu.SemaphoreType.DMA
    block = (CHUNKS, LINE, HALF, SHARE, LANES)
    held = (BANDS, DEPTH * OWNERS, 8, LANES)
    return pl.pallas_call(
        kernel,
        out_shape=pltpu.VMEM((KEEP,) + interferograms.shape[1:], f32),
        in_specs=[pl.BlockSpec(memory_space=pltpu.HBM), pl.BlockSpec(memory_space=pltpu.VMEM)],
        out_specs=pl.BlockSpec(memory_space=pltpu.VMEM),
        scratch_shapes=[
            pltpu.VMEM(held, f32),
            pltpu.VMEM((WHOLE // 2,) + held[1:], f32),
            pltpu.VMEM(block, f32),
            pltpu.VMEM((2,) + block, f32),
            pltpu.VMEM((BANDS, SHARE, 8, LANES), f32),
            pltpu.VMEM((BANDS + 2, OWNERS, KEEP, 8, LANES), f32),
            pltpu.VMEM((PAD, 1024), bf16),
            pltpu.VMEM((2 * PAD, PAD), f32),
            pltpu.VMEM((ND, 2 * LANES), bf16),
            pltpu.VMEM((ND, LANES), bf16),
            pltpu.VMEM((ND, 2 * LANES), bf16),
            pltpu.VMEM((ND, LANES), bf16),
            dma, dma((CHUNKS,)),
            dma, dma((UNITS,)),
            dma((2,)), dma((UNITS, LINE + 1)),
            dma, dma((BANDS,)),
            dma((2,)), dma((2,)),
            pltpu.SemaphoreType.REGULAR, pltpu.SemaphoreType.REGULAR,
            pltpu.VMEM((OWNERS, KEEP, 8, LANES), f32), dma, dma,
        ],
        compiler_params=pltpu.CompilerParams(
            collective_id=0, has_side_effects=True, vmem_limit_bytes=61 * 1024 * 1024
        ),
    )(interferograms, pairs.T)


def solution(mesh):
    return jax.shard_map(
        shards,
        mesh=mesh,
        in_specs=(P("stack", "rows", None), P()),
        out_specs=P("stack", "rows", None),
        check_vma=False,
    )
```
